128 devices in a mesh: rep: 8 (over z, core), fsdp: 16 (over y, x).
Axes of the slice: x: 4, y: 4, z: 4, core: 2. Of those that a mesh axis runs over, the one named last changes fastest.
Arguments:
- gradient: bfloat16 [8, 4, 128, 13824], P('rep', None, 'fsdp'), may hold values from -6 to 6
- momentum: float32 [8, 4, 128, 13824], P('rep', None, 'fsdp'), may hold values from -6 to 6
- params: bfloat16 [4, 128, 13824], P(None, 'fsdp'), may hold values from -6 to 6
- bands: int32 [8, 4, 128, 216, 2], P('rep', None, 'fsdp'), may hold values from 0 to 7, as said below
Outputs:
- new_momentum: float32 [8, 4, 128, 13824], P('rep', None, 'fsdp')
- new_params: bfloat16 [4, 128, 13824], replicated
The draws below stay inside these ranges and needn't reach their ends.
Inputs may be any that keep to these rules, and one draw needn't show every extreme that they name: The 2 bands of one block of one replica differ.
All inputs are finite; a program needn't handle non-finite values.
Results may differ from the reference program's by a relative error of at most 0.0059.
Values may be sent and summed in bfloat16 or wider, within the bound.
No kernel may reach another device: no remote copies, remote signals or barrier semaphores. Data moves between devices by JAX's collectives and lax.ppermute only.
A program may use at most 256 MiB of HBM per device.

```python
import math
import jax
import jax.numpy as jnp
from jax import lax

FF = 13824
LAYERS = 4
GROUP = 64
BANDS = 8
SELECT = 2
GROUPS = 216
ROWS = 128
N_REP = 8


def draw_bands(key, part):
    key = jax.random.fold_in(key, 5)
    shape = (N_REP, LAYERS, ROWS, GROUPS, BANDS)
    scores = jax.random.randint(key, shape, 0, 1 << 20) * BANDS + jnp.arange(BANDS).astype(jnp.int32)
    ignored, picked = lax.top_k(scores, SELECT)
    return picked.astype(jnp.int32)


def steps_of(key, shape, pieces, least, high):
    def one(axis_at, shards_of):
        steps = jax.random.uniform(jax.random.fold_in(jax.random.fold_in(key, 6), axis_at), (shards_of,), jnp.float32, least / len(pieces), high / len(pieces))
        return jnp.repeat(jnp.exp(steps), shape[axis_at] // shards_of).reshape((-1,) + (1,) * (len(shape) - axis_at - 1))

    gain = one(*pieces[0])
    for cut in pieces[1:]:
        gain = gain * one(*cut)
    return gain


def normal_values(rng, dims, spread, reach, cuts=(), kind=jnp.bfloat16):
    result = jax.random.normal(rng, dims, jnp.float32) * spread
    if len(cuts) > 0:
        result = steps_of(rng, dims, cuts, -0.22, 0.18) * result
    return jnp.clip(result, min=-reach, max=reach).astype(kind)


def setup_inputs(seed: int = 0) -> dict:
    streams_of = jax.random.split(jax.random.key(seed), 5)
    gradient = normal_values(streams_of[0], (N_REP, LAYERS, ROWS, FF), 1.0, 6.0, ((0, 8), (2, 16)))
    momentum = normal_values(streams_of[1], (N_REP, LAYERS, ROWS, FF), 1.0, 6.0, ((0, 8), (2, 16)), jnp.float32)
    params = normal_values(streams_of[2], (LAYERS, ROWS, FF), 1.0, 6.0, ((1, 16),))
    bands = draw_bands(jax.random.fold_in(streams_of[4], 71), 0)
    return {"gradient": gradient, "momentum": momentum, "params": params, "bands": bands}


decay_rate = 0.9
step_size = 1.0

def cosine_table():
    freqs = jnp.arange(GROUP).astype(jnp.float32)
    samples = jnp.arange(GROUP).astype(jnp.float32)
    scales = jnp.where(freqs == 0, math.sqrt(1.0 / GROUP), math.sqrt(2.0 / GROUP))
    return scales[:, None] * jnp.cos(math.pi * (2.0 * samples[None, :] + 1.0) * freqs[:, None] / (2.0 * GROUP))

def reference(gradient, momentum, params, bands):
    cosines = cosine_table()
    highest = lax.Precision.HIGHEST
    merged = decay_rate * momentum + gradient.astype(jnp.float32)
    grouped = merged.reshape(N_REP, LAYERS, ROWS, GROUPS, GROUP)
    spectra = jnp.einsum('alrcn,kn->alrck', grouped, cosines, precision=highest)
    banded = spectra.reshape(N_REP, LAYERS, ROWS, GROUPS, BANDS, 8)
    chosen = (bands[..., None] == jnp.arange(BANDS).astype(jnp.int32)).astype(jnp.float32)
    picked = jnp.einsum('alrcsb,alrcbj->alrcsj', chosen, banded, precision=highest)
    kept_mask = lax.optimization_barrier(jnp.sum(chosen, axis=4))
    remain = banded * (1.0 - kept_mask[..., None])
    new_momentum = jnp.einsum('alrck,kn->alrcn', remain.reshape(N_REP, LAYERS, ROWS, GROUPS, GROUP), cosines, precision=highest)
    new_momentum = new_momentum.reshape(N_REP, LAYERS, ROWS, FF)
    restored = jnp.einsum('alrcsb,alrcsj->lrcbj', chosen, picked, precision=highest) / N_REP
    decoded = jnp.einsum('lrck,kn->lrcn', restored.reshape(LAYERS, ROWS, GROUPS, GROUP), cosines, precision=highest)
    decoded = decoded.reshape(LAYERS, ROWS, FF)
    new_params = (params.astype(jnp.float32) - step_size * decoded).astype(jnp.bfloat16)
    return (new_momentum, new_params)
```

```python
import math

import jax
import jax.numpy as jnp
import numpy as np
from jax import lax
from jax.experimental import pallas as pl
from jax.experimental.pallas import tpu as pltpu
from jax.sharding import PartitionSpec as P

GROUP = 64
BANDS = 8
LAYERS = 4
ROWS_HERE = 8
WIDTH = 13824
HALF = WIDTH // 2
QUARTER = HALF // 2
WIDE = 256
LANES = 128
REPS = 8

decay_rate = 0.9
step_size = 1.0
VMEM_LIMIT = 48 * 1024 * 1024


def cosine_table():
    k = np.arange(GROUP, dtype=np.float64)
    n = np.arange(GROUP, dtype=np.float64)
    scale = np.where(k == 0, math.sqrt(1.0 / GROUP), math.sqrt(2.0 / GROUP))
    return scale[:, None] * np.cos(math.pi * (2.0 * n[None, :] + 1.0) * k[:, None] / (2.0 * GROUP))


def split_table(table):
    high = jnp.asarray(table, jnp.float32).astype(jnp.bfloat16)
    low = (jnp.asarray(table, jnp.float32) - high.astype(jnp.float32)).astype(jnp.bfloat16)
    return jnp.stack([high, low])


def dot3(x, table_ref):
    high = x.astype(jnp.bfloat16)
    low = (x - high.astype(jnp.float32)).astype(jnp.bfloat16)
    total = jnp.dot(high, table_ref[1], preferred_element_type=jnp.float32)
    total += jnp.dot(low, table_ref[0], preferred_element_type=jnp.float32)
    return total + jnp.dot(high, table_ref[0], preferred_element_type=jnp.float32)


def stacked(x):
    return jnp.concatenate([x[:, at : at + WIDE] for at in range(0, x.shape[1], WIDE)], axis=0)


def merge_and_pick(bands_ref, gradient_ref, momentum_ref, forward_ref):
    merged = decay_rate * momentum_ref[0, 0] + gradient_ref[0, 0].astype(jnp.float32)
    merged = stacked(merged)
    spectra = dot3(merged, forward_ref)
    lane = lax.broadcasted_iota(jnp.int32, (ROWS_HERE, LANES), 1)
    upper = lax.shift_right_logical(lane, 6)
    band = lax.bitwise_and(lax.shift_right_logical(lane, 3), 7)
    tiles = []
    for tile in range(WIDTH // LANES):
        part = tile // 64
        index = upper + (2 * tile - LANES * part)
        first = jnp.take_along_axis(bands_ref[0, 0, :, part * LANES : (part + 1) * LANES], index, axis=1)
        second = jnp.take_along_axis(bands_ref[0, 1, :, part * LANES : (part + 1) * LANES], index, axis=1)
        row = (tile // 2) * ROWS_HERE
        column = (tile % 2) * LANES
        values = spectra[row : row + ROWS_HERE, column : column + LANES]
        tiles.append(jnp.where((first == band) | (second == band), values, 0.0))
    return merged, tiles


def pick_kernel(bands_ref, gradient_ref, momentum_ref, forward_ref, picked_ref):
    _, tiles = merge_and_pick(bands_ref, gradient_ref, momentum_ref, forward_ref)
    for tile, values in enumerate(tiles):
        side, at = divmod(tile, HALF // LANES)
        picked_ref[side, :, at * LANES : (at + 1) * LANES] = values.astype(jnp.bfloat16)


def momentum_kernel(bands_ref, gradient_ref, momentum_ref, forward_ref, inverse_ref, out_ref):
    merged, tiles = merge_and_pick(bands_ref, gradient_ref, momentum_ref, forward_ref)
    wide = [jnp.concatenate(tiles[at : at + 2], axis=1) for at in range(0, len(tiles), 2)]
    kept = merged - dot3(jnp.concatenate(wide, axis=0), inverse_ref)
    for at in range(WIDTH // WIDE):
        out_ref[0, 0, :, at * WIDE : (at + 1) * WIDE] = kept[at * ROWS_HERE : (at + 1) * ROWS_HERE]


def decode_kernel(place_ref, received_ref, params_ref, inverse_ref, out_ref):
    del place_ref
    total = received_ref[0].astype(jnp.float32)
    for replica in range(1, REPS):
        total += received_ref[replica].astype(jnp.float32)
    restored = stacked(total * (1.0 / REPS))
    restored = jnp.concatenate([restored, jnp.zeros((ROWS_HERE, WIDE), jnp.float32)], axis=0)
    decoded = dot3(restored, inverse_ref)
    for at in range(HALF // WIDE):
        before = params_ref[0, :, at * WIDE : (at + 1) * WIDE].astype(jnp.float32)
        after = before - step_size * decoded[at * ROWS_HERE : (at + 1) * ROWS_HERE]
        after = after.astype(jnp.bfloat16)
        for part in range(2):
            column = at * WIDE + part * LANES
            side, column = divmod(column, QUARTER)
            out_ref[side, :, column : column + LANES] = after[:, part * LANES : (part + 1) * LANES]


def copy_all(pairs, sems):
    copies = [pltpu.make_async_copy(src, dst, sems.at[i]) for i, (src, dst) in enumerate(pairs)]
    for copy in copies:
        copy.start()
    for copy in copies:
        copy.wait()


def bring_together(place, blocks, which, out_shapes, targets):
    def kernel(place_ref, *refs):
        ins, outs, sems = refs[: len(blocks)], refs[len(blocks) : -1], refs[-1]
        pairs = []
        for k, block in enumerate(ins):
            source = lax.rem(place_ref[which] + (4 - k), 4)
            pairs += targets(outs, block, source)
        copy_all(pairs, sems)

    count = len(blocks) * len(out_shapes)
    return pl.pallas_call(
        kernel,
        out_shape=out_shapes,
        in_specs=[pl.BlockSpec(memory_space=pltpu.SMEM)] + [pl.BlockSpec(memory_space=pl.ANY)] * len(blocks),
        out_specs=[pl.BlockSpec(memory_space=pl.ANY)] * len(out_shapes),
        scratch_shapes=[pltpu.SemaphoreType.DMA((count,))],
        cost_estimate=pl.CostEstimate(flops=0, bytes_accessed=2 * sum(b.size * 2 for b in blocks), transcendentals=0),
    )(place, *blocks)


def write_blocks(place, whole, items):
    blocks = [item[0] for item in items]

    def kernel(place_ref, *refs):
        ins, out, sems = refs[: len(blocks)], refs[-2], refs[-1]
        y, x, core = place_ref[1], place_ref[2], place_ref[3]
        pairs = []
        for block, (_, axis, first, steps, other) in zip(ins, items):
            side = core if other == 0 else 1 - core
            layers = pl.ds(first, 2)
            if axis == "y":
                column = pl.multiple_of(side * HALF, LANES)
                target = out.at[layers, lax.rem(y + (4 - steps), 4), :, :, pl.ds(column, QUARTER)]
            else:
                column = pl.multiple_of(side * HALF + QUARTER, LANES)
                target = out.at[layers, :, lax.rem(x + (4 - steps), 4), :, pl.ds(column, QUARTER)]
            pairs.append((block, target))
        copy_all(pairs, sems)

    any_space = pl.BlockSpec(memory_space=pl.ANY)
    operands = [place] + blocks
    specs = [pl.BlockSpec(memory_space=pltpu.SMEM)] + [any_space] * len(blocks)
    aliases = {}
    if whole is not None:
        aliases = {len(operands): 0}
        operands.append(whole)
        specs.append(any_space)
    return pl.pallas_call(
        kernel,
        out_shape=jax.ShapeDtypeStruct((LAYERS, 4, 4, ROWS_HERE, WIDTH), jnp.bfloat16),
        in_specs=specs,
        out_specs=any_space,
        scratch_shapes=[pltpu.SemaphoreType.DMA((len(blocks),))],
        input_output_aliases=aliases,
        cost_estimate=pl.CostEstimate(flops=0, bytes_accessed=2 * sum(b.size * 2 for b in blocks), transcendentals=0),
    )(*operands)


def shift_z(x, steps):
    return lax.ppermute(x, "rep", [(r, (r + 2 * steps) % 8) for r in range(8)])


def shift_core(x):
    return lax.ppermute(x, "rep", [(r, r ^ 1) for r in range(8)])


def shift_plane(x, axis, steps):
    pairs = []
    for y in range(4):
        for u in range(4):
            if axis == "y":
                pairs.append((y * 4 + u, (y + steps) % 4 * 4 + u))
            else:
                pairs.append((y * 4 + u, y * 4 + (u + steps) % 4))
    return lax.ppermute(x, "fsdp", pairs)


def shards(gradient, momentum, params, bands):
    rep, fsdp = lax.axis_index("rep"), lax.axis_index("fsdp")
    place = jnp.stack([rep // 2, fsdp // 4, fsdp % 4, rep % 2]).astype(jnp.int32)
    table = cosine_table()
    forward = split_table(np.kron(np.eye(WIDE // GROUP), table.T))
    inverse = split_table(np.kron(np.eye(WIDE // GROUP), table))
    blocks = WIDTH // GROUP
    by_layer = jnp.pad(jnp.transpose(bands[0], (0, 3, 1, 2)), ((0, 0), (0, 0), (0, 0), (0, WIDE - blocks)))

    row_spec = pl.BlockSpec((1, 1, ROWS_HERE, WIDTH), lambda l: (0, l, 0, 0))
    bands_spec = pl.BlockSpec((1, 2, ROWS_HERE, WIDE), lambda l: (l, 0, 0, 0))
    table_spec = pl.BlockSpec((2, WIDE, WIDE), lambda l: (0, 0, 0))
    dot_flops = 2 * 3 * LAYERS * ROWS_HERE * WIDTH * WIDE
    picked = pl.pallas_call(
        pick_kernel,
        grid=(LAYERS,),
        in_specs=[bands_spec, row_spec, row_spec, table_spec],
        out_specs=pl.BlockSpec((2, ROWS_HERE, HALF), lambda l: (l, 0, 0)),
        out_shape=jax.ShapeDtypeStruct((REPS, ROWS_HERE, HALF), jnp.bfloat16),
        compiler_params=pltpu.CompilerParams(vmem_limit_bytes=VMEM_LIMIT),
        cost_estimate=pl.CostEstimate(flops=dot_flops, bytes_accessed=4 * 1024 * 1024, transcendentals=0),
    )(by_layer, gradient, momentum, forward)
    received = lax.all_to_all(picked, "rep", 0, 0, tiled=True)

    piece = pl.pallas_call(
        decode_kernel,
        grid_spec=pltpu.PrefetchScalarGridSpec(
            num_scalar_prefetch=1,
            grid=(1,),
            in_specs=[
                pl.BlockSpec((REPS, ROWS_HERE, HALF), lambda i, at: (0, 0, 0)),
                pl.BlockSpec((1, ROWS_HERE, HALF), lambda i, at: (at[0], 0, at[3])),
                pl.BlockSpec((2, WIDE, WIDE), lambda i, at: (0, 0, 0)),
            ],
            out_specs=pl.BlockSpec((2, ROWS_HERE, QUARTER), lambda i, at: (0, 0, 0)),
        ),
        out_shape=jax.ShapeDtypeStruct((2, ROWS_HERE, QUARTER), jnp.bfloat16),
        compiler_params=pltpu.CompilerParams(vmem_limit_bytes=VMEM_LIMIT),
    )(place, received, params, inverse)

    along_z = [piece] + [shift_z(piece, k) for k in (1, 2, 3)]
    part = jax.ShapeDtypeStruct((LAYERS, ROWS_HERE, QUARTER), jnp.bfloat16)
    x_first, y_first = bring_together(
        place, along_z, 0, [part, part],
        lambda outs, block, source: [(block.at[side], outs[side].at[source]) for side in range(2)],
    )
    x_blocks = [x_first] + [shift_plane(x_first, "x", k) for k in (1, 2, 3)]
    y_blocks = [y_first] + [shift_plane(y_first, "y", k) for k in (1, 2, 3)]
    unit = jax.ShapeDtypeStruct((2, 4, ROWS_HERE, QUARTER), jnp.bfloat16)

    def by_halves(outs, block, source):
        return [(block.at[pl.ds(2 * i, 2)], outs[i].at[:, source]) for i in range(2)]

    x_units = bring_together(place, x_blocks, 2, [unit, unit], by_halves)
    y_units = bring_together(place, y_blocks, 1, [unit, unit], by_halves)

    own, near, far = [], [], []
    for axis, units in (("y", x_units), ("x", y_units)):
        for i, block in enumerate(units):
            own.append((block, axis, 2 * i, 0))
            before = shift_plane(block, axis, 1)
            after = shift_plane(block, axis, 3)
            near.append((before, axis, 2 * i, 1))
            near.append((after, axis, 2 * i, 3))
            onward = shift_plane(before, axis, 1) if i == 0 else shift_plane(after, axis, 3)
            far.append((onward, axis, 2 * i, 2))

    whole = None
    for group in (own, near, far):
        items = [item + (0,) for item in group] + [(shift_core(item[0]),) + item[1:] + (1,) for item in group]
        whole = write_blocks(place, whole, items)

    new_momentum = pl.pallas_call(
        momentum_kernel,
        grid=(LAYERS,),
        in_specs=[bands_spec, row_spec, row_spec, table_spec, table_spec],
        out_specs=row_spec,
        out_shape=jax.ShapeDtypeStruct(momentum.shape, jnp.float32),
        compiler_params=pltpu.CompilerParams(vmem_limit_bytes=VMEM_LIMIT),
        cost_estimate=pl.CostEstimate(flops=2 * dot_flops, bytes_accessed=6 * 1024 * 1024, transcendentals=0),
    )(by_layer, gradient, momentum, forward, inverse)
    return new_momentum, whole.reshape(LAYERS, 16 * ROWS_HERE, WIDTH)


def solution(mesh):
    in_specs = (
        P("rep", None, "fsdp", None),
        P("rep", None, "fsdp", None),
        P(None, "fsdp", None),
        P("rep", None, "fsdp", None, None),
    )
    out_specs = (P("rep", None, "fsdp", None), P())
    return jax.shard_map(shards, mesh=mesh, in_specs=in_specs, out_specs=out_specs, check_vma=False)
```

```python
import math

import jax
import jax.numpy as jnp
import numpy as np
from jax import lax
from jax.experimental import pallas as pl
from jax.experimental.pallas import tpu as pltpu
from jax.sharding import PartitionSpec as P

GROUP = 64
BANDS = 8
LAYERS = 4
ROWS_HERE = 8
WIDTH = 13824
HALF = WIDTH // 2
QUARTER = HALF // 2
WIDE = 256
LANES = 128
REPS = 8

decay_rate = 0.9
step_size = 1.0
VMEM_LIMIT = 16 * 1024 * 1024


def cosine_table():
    k = np.arange(GROUP, dtype=np.float64)
    n = np.arange(GROUP, dtype=np.float64)
    scale = np.where(k == 0, math.sqrt(1.0 / GROUP), math.sqrt(2.0 / GROUP))
    return scale[:, None] * np.cos(math.pi * (2.0 * n[None, :] + 1.0) * k[:, None] / (2.0 * GROUP))


def split_table(table):
    high = jnp.asarray(table, jnp.float32).astype(jnp.bfloat16)
    low = (jnp.asarray(table, jnp.float32) - high.astype(jnp.float32)).astype(jnp.bfloat16)
    return jnp.stack([high, low])


def dot3(x, table_ref):
    high = x.astype(jnp.bfloat16)
    low = (x - high.astype(jnp.float32)).astype(jnp.bfloat16)
    total = jnp.dot(high, table_ref[1], preferred_element_type=jnp.float32)
    total += jnp.dot(low, table_ref[0], preferred_element_type=jnp.float32)
    return total + jnp.dot(high, table_ref[0], preferred_element_type=jnp.float32)


def stacked(x):
    return jnp.concatenate([x[:, at : at + WIDE] for at in range(0, x.shape[1], WIDE)], axis=0)


def merge_and_pick(bands_ref, gradient_ref, momentum_ref, forward_ref):
    merged = decay_rate * momentum_ref[0, 0] + gradient_ref[0, 0].astype(jnp.float32)
    merged = stacked(merged)
    spectra = dot3(merged, forward_ref)
    lane = lax.broadcasted_iota(jnp.int32, (ROWS_HERE, LANES), 1)
    upper = lax.shift_right_logical(lane, 6)
    band = lax.bitwise_and(lax.shift_right_logical(lane, 3), 7)
    tiles = []
    for tile in range(WIDTH // LANES):
        part = tile // 64
        index = upper + (2 * tile - LANES * part)
        first = jnp.take_along_axis(bands_ref[0, 0, :, part * LANES : (part + 1) * LANES], index, axis=1)
        second = jnp.take_along_axis(bands_ref[0, 1, :, part * LANES : (part + 1) * LANES], index, axis=1)
        row = (tile // 2) * ROWS_HERE
        column = (tile % 2) * LANES
        values = spectra[row : row + ROWS_HERE, column : column + LANES]
        tiles.append(jnp.where((first == band) | (second == band), values, 0.0))
    return merged, tiles


def pick_kernel(bands_ref, gradient_ref, momentum_ref, forward_ref, picked_ref):
    _, tiles = merge_and_pick(bands_ref, gradient_ref, momentum_ref, forward_ref)
    for tile, values in enumerate(tiles):
        side, at = divmod(tile, HALF // LANES)
        picked_ref[side, :, at * LANES : (at + 1) * LANES] = values.astype(jnp.bfloat16)


def momentum_kernel(bands_ref, gradient_ref, momentum_ref, forward_ref, inverse_ref, out_ref):
    merged, tiles = merge_and_pick(bands_ref, gradient_ref, momentum_ref, forward_ref)
    wide = [jnp.concatenate(tiles[at : at + 2], axis=1) for at in range(0, len(tiles), 2)]
    kept = merged - dot3(jnp.concatenate(wide, axis=0), inverse_ref)
    for at in range(WIDTH // WIDE):
        out_ref[0, 0, :, at * WIDE : (at + 1) * WIDE] = kept[at * ROWS_HERE : (at + 1) * ROWS_HERE]


def decode_kernel(place_ref, received_ref, params_ref, inverse_ref, out_ref):
    del place_ref
    total = received_ref[0].astype(jnp.float32)
    for replica in range(1, REPS):
        total += received_ref[replica].astype(jnp.float32)
    restored = stacked(total * (1.0 / REPS))
    restored = jnp.concatenate([restored, jnp.zeros((ROWS_HERE, WIDE), jnp.float32)], axis=0)
    decoded = dot3(restored, inverse_ref)
    for at in range(HALF // WIDE):
        before = params_ref[0, :, at * WIDE : (at + 1) * WIDE].astype(jnp.float32)
        after = before - step_size * decoded[at * ROWS_HERE : (at + 1) * ROWS_HERE]
        after = after.astype(jnp.bfloat16)
        for part in range(2):
            column = at * WIDE + part * LANES
            side, column = divmod(column, QUARTER)
            out_ref[side, :, column : column + LANES] = after[:, part * LANES : (part + 1) * LANES]


def copy_all(pairs, sems):
    copies = [pltpu.make_async_copy(src, dst, sems.at[i]) for i, (src, dst) in enumerate(pairs)]
    for copy in copies:
        copy.start()
    for copy in copies:
        copy.wait()


def bring_together(place, blocks, which, out_shapes, targets):
    def kernel(place_ref, *refs):
        ins, outs = refs[: len(blocks)], refs[len(blocks) :]
        for k, block in enumerate(ins):
            source = lax.rem(place_ref[which] + (4 - k), 4)
            for src, dst in targets(outs, block, source):
                dst[...] = src[...]

    vmem = pl.BlockSpec(memory_space=pltpu.VMEM)
    return pl.pallas_call(
        kernel,
        out_shape=out_shapes,
        in_specs=[pl.BlockSpec(memory_space=pltpu.SMEM)] + [vmem] * len(blocks),
        out_specs=[vmem] * len(out_shapes),
        compiler_params=pltpu.CompilerParams(vmem_limit_bytes=VMEM_LIMIT),
        cost_estimate=pl.CostEstimate(flops=0, bytes_accessed=2 * sum(b.size * 2 for b in blocks), transcendentals=0),
    )(place, *blocks)


def write_blocks(place, whole, items):
    blocks = [item[0] for item in items]

    def kernel(place_ref, *refs):
        ins, out, sems = refs[: len(blocks)], refs[-2], refs[-1]
        y, x, core = place_ref[1], place_ref[2], place_ref[3]
        pairs = []
        for block, (_, axis, first, steps, other) in zip(ins, items):
            side = core if other == 0 else 1 - core
            layers = pl.ds(first, 2)
            if axis == "y":
                column = pl.multiple_of(side * HALF, LANES)
                target = out.at[layers, lax.rem(y + (4 - steps), 4), :, :, pl.ds(column, QUARTER)]
            else:
                column = pl.multiple_of(side * HALF + QUARTER, LANES)
                target = out.at[layers, :, lax.rem(x + (4 - steps), 4), :, pl.ds(column, QUARTER)]
            pairs.append((block, target))
        copy_all(pairs, sems)

    any_space = pl.BlockSpec(memory_space=pl.ANY)
    operands = [place] + blocks
    specs = [pl.BlockSpec(memory_space=pltpu.SMEM)] + [pl.BlockSpec(memory_space=pltpu.VMEM)] * len(blocks)
    aliases = {}
    if whole is not None:
        aliases = {len(operands): 0}
        operands.append(whole)
        specs.append(any_space)
    return pl.pallas_call(
        kernel,
        out_shape=jax.ShapeDtypeStruct((LAYERS, 4, 4, ROWS_HERE, WIDTH), jnp.bfloat16),
        in_specs=specs,
        out_specs=any_space,
        scratch_shapes=[pltpu.SemaphoreType.DMA((len(blocks),))],
        input_output_aliases=aliases,
        compiler_params=pltpu.CompilerParams(vmem_limit_bytes=VMEM_LIMIT),
        cost_estimate=pl.CostEstimate(flops=0, bytes_accessed=2 * sum(b.size * 2 for b in blocks), transcendentals=0),
    )(*operands)


def shift_z(x, steps):
    return lax.ppermute(x, "rep", [(r, (r + 2 * steps) % 8) for r in range(8)])


def shift_core(x):
    return lax.ppermute(x, "rep", [(r, r ^ 1) for r in range(8)])


def shift_plane(x, axis, steps):
    pairs = []
    for y in range(4):
        for u in range(4):
            if axis == "y":
                pairs.append((y * 4 + u, (y + steps) % 4 * 4 + u))
            else:
                pairs.append((y * 4 + u, y * 4 + (u + steps) % 4))
    return lax.ppermute(x, "fsdp", pairs)


def shards(gradient, momentum, params, bands):
    rep, fsdp = lax.axis_index("rep"), lax.axis_index("fsdp")
    place = jnp.stack([rep // 2, fsdp // 4, fsdp % 4, rep % 2]).astype(jnp.int32)
    table = cosine_table()
    forward = split_table(np.kron(np.eye(WIDE // GROUP), table.T))
    inverse = split_table(np.kron(np.eye(WIDE // GROUP), table))
    blocks = WIDTH // GROUP
    by_layer = jnp.pad(jnp.transpose(bands[0], (0, 3, 1, 2)), ((0, 0), (0, 0), (0, 0), (0, WIDE - blocks)))

    row_spec = pl.BlockSpec((1, 1, ROWS_HERE, WIDTH), lambda l: (0, l, 0, 0))
    bands_spec = pl.BlockSpec((1, 2, ROWS_HERE, WIDE), lambda l: (l, 0, 0, 0))
    table_spec = pl.BlockSpec((2, WIDE, WIDE), lambda l: (0, 0, 0))
    dot_flops = 2 * 3 * LAYERS * ROWS_HERE * WIDTH * WIDE
    picked = pl.pallas_call(
        pick_kernel,
        grid=(LAYERS,),
        in_specs=[bands_spec, row_spec, row_spec, table_spec],
        out_specs=pl.BlockSpec((2, ROWS_HERE, HALF), lambda l: (l, 0, 0)),
        out_shape=jax.ShapeDtypeStruct((REPS, ROWS_HERE, HALF), jnp.bfloat16),
        compiler_params=pltpu.CompilerParams(vmem_limit_bytes=VMEM_LIMIT),
        cost_estimate=pl.CostEstimate(flops=dot_flops, bytes_accessed=4 * 1024 * 1024, transcendentals=0),
    )(by_layer, gradient, momentum, forward)
    received = lax.all_to_all(picked, "rep", 0, 0, tiled=True)

    piece = pl.pallas_call(
        decode_kernel,
        grid_spec=pltpu.PrefetchScalarGridSpec(
            num_scalar_prefetch=1,
            grid=(1,),
            in_specs=[
                pl.BlockSpec((REPS, ROWS_HERE, HALF), lambda i, at: (0, 0, 0)),
                pl.BlockSpec((1, ROWS_HERE, HALF), lambda i, at: (at[0], 0, at[3])),
                pl.BlockSpec((2, WIDE, WIDE), lambda i, at: (0, 0, 0)),
            ],
            out_specs=pl.BlockSpec((2, ROWS_HERE, QUARTER), lambda i, at: (0, 0, 0)),
        ),
        out_shape=jax.ShapeDtypeStruct((2, ROWS_HERE, QUARTER), jnp.bfloat16),
        compiler_params=pltpu.CompilerParams(vmem_limit_bytes=VMEM_LIMIT),
    )(place, received, params, inverse)

    along_z = [piece] + [shift_z(piece, k) for k in (1, 2, 3)]
    part = jax.ShapeDtypeStruct((LAYERS, ROWS_HERE, QUARTER), jnp.bfloat16)
    x_first, y_first = bring_together(
        place, along_z, 0, [part, part],
        lambda outs, block, source: [(block.at[side], outs[side].at[source]) for side in range(2)],
    )
    x_blocks = [x_first] + [shift_plane(x_first, "x", k) for k in (1, 2, 3)]
    y_blocks = [y_first] + [shift_plane(y_first, "y", k) for k in (1, 2, 3)]
    unit = jax.ShapeDtypeStruct((2, 4, ROWS_HERE, QUARTER), jnp.bfloat16)

    def by_halves(outs, block, source):
        return [(block.at[pl.ds(2 * i, 2)], outs[i].at[:, source]) for i in range(2)]

    x_units = bring_together(place, x_blocks, 2, [unit, unit], by_halves)
    y_units = bring_together(place, y_blocks, 1, [unit, unit], by_halves)

    own, near, far = [], [], []
    for axis, units in (("y", x_units), ("x", y_units)):
        for i, block in enumerate(units):
            own.append((block, axis, 2 * i, 0))
            before = shift_plane(block, axis, 1)
            after = shift_plane(block, axis, 3)
            near.append((before, axis, 2 * i, 1))
            near.append((after, axis, 2 * i, 3))
            onward = shift_plane(before, axis, 1) if i == 0 else shift_plane(after, axis, 3)
            far.append((onward, axis, 2 * i, 2))

    whole = None
    for group in (own, near, far):
        items = [item + (0,) for item in group] + [(shift_core(item[0]),) + item[1:] + (1,) for item in group]
        whole = write_blocks(place, whole, items)

    new_momentum = pl.pallas_call(
        momentum_kernel,
        grid=(LAYERS,),
        in_specs=[bands_spec, row_spec, row_spec, table_spec, table_spec],
        out_specs=row_spec,
        out_shape=jax.ShapeDtypeStruct(momentum.shape, jnp.float32),
        compiler_params=pltpu.CompilerParams(vmem_limit_bytes=VMEM_LIMIT),
        cost_estimate=pl.CostEstimate(flops=2 * dot_flops, bytes_accessed=6 * 1024 * 1024, transcendentals=0),
    )(by_layer, gradient, momentum, forward, inverse)
    return new_momentum, whole.reshape(LAYERS, 16 * ROWS_HERE, WIDTH)


def solution(mesh):
    in_specs = (
        P("rep", None, "fsdp", None),
        P("rep", None, "fsdp", None),
        P(None, "fsdp", None),
        P("rep", None, "fsdp", None, None),
    )
    out_specs = (P("rep", None, "fsdp", None), P())
    return jax.shard_map(shards, mesh=mesh, in_specs=in_specs, out_specs=out_specs, check_vma=False)
```

```python
import math

import jax
import jax.numpy as jnp
import numpy as np
from jax import lax
from jax.experimental import pallas as pl
from jax.experimental.pallas import tpu as pltpu
from jax.sharding import PartitionSpec as P

GROUP = 64
BANDS = 8
LAYERS = 4
ROWS_HERE = 8
WIDTH = 13824
HALF = WIDTH // 2
WIDE = 256
LANES = 128
REPS = 8
UNIT = 2
UNITS = LAYERS // UNIT

decay_rate = 0.9
step_size = 1.0
VMEM_LIMIT = 16 * 1024 * 1024


def cosine_table():
    k = np.arange(GROUP, dtype=np.float64)
    n = np.arange(GROUP, dtype=np.float64)
    scale = np.where(k == 0, math.sqrt(1.0 / GROUP), math.sqrt(2.0 / GROUP))
    return scale[:, None] * np.cos(math.pi * (2.0 * n[None, :] + 1.0) * k[:, None] / (2.0 * GROUP))


def split_table(table):
    high = jnp.asarray(table, jnp.float32).astype(jnp.bfloat16)
    low = (jnp.asarray(table, jnp.float32) - high.astype(jnp.float32)).astype(jnp.bfloat16)
    return jnp.stack([high, low])


def dot3(x, table_ref):
    high = x.astype(jnp.bfloat16)
    low = (x - high.astype(jnp.float32)).astype(jnp.bfloat16)
    total = jnp.dot(high, table_ref[1], preferred_element_type=jnp.float32)
    total += jnp.dot(low, table_ref[0], preferred_element_type=jnp.float32)
    return total + jnp.dot(high, table_ref[0], preferred_element_type=jnp.float32)


def stacked(x):
    return jnp.concatenate([x[:, at : at + WIDE] for at in range(0, x.shape[1], WIDE)], axis=0)


def pick_tiles(bands_ref, side, layers, spectra):
    lane = lax.broadcasted_iota(jnp.int32, (ROWS_HERE, LANES), 1)
    upper = lax.shift_right_logical(lane, 6)
    band = lax.bitwise_and(lax.shift_right_logical(lane, 3), 7)
    tiles = {}
    for i, layer in enumerate(layers):
        first_bands = bands_ref[layer, 0, side]
        second_bands = bands_ref[layer, 1, side]
        for tile in range(HALF // LANES):
            index = upper + 2 * tile
            first = jnp.take_along_axis(first_bands, index, axis=1)
            second = jnp.take_along_axis(second_bands, index, axis=1)
            row = (i * (HALF // WIDE) + tile // 2) * ROWS_HERE
            column = (tile % 2) * LANES
            values = spectra[row : row + ROWS_HERE, column : column + LANES]
            tiles[i, tile] = jnp.where((first == band) | (second == band), values, 0.0)
    return tiles


def merged_rows(gradient, momentum):
    merged = decay_rate * momentum + gradient.astype(jnp.float32)
    return jnp.concatenate([stacked(merged[i]) for i in range(merged.shape[0])], axis=0)


HBM = pl.BlockSpec(memory_space=pltpu.HBM)
VMEM = pl.BlockSpec(memory_space=pltpu.VMEM)
SMEM = pl.BlockSpec(memory_space=pltpu.SMEM)
HALF_UNIT = jax.ShapeDtypeStruct((UNIT, ROWS_HERE, HALF), jnp.bfloat16)


def cost(flops, size):
    return pl.CostEstimate(flops=flops, bytes_accessed=size, transcendentals=0)


def pick(place, by_layer, gradient, momentum, forward, units, own, received=None, params=None, inverse=None):
    count = len(units)
    extra = ([] if received is None else [received]) + ([] if params is None else [params]) + ([] if inverse is None else [inverse])
    n_extra = len(extra)
    out_shapes = [HALF_UNIT] * count
    if params is not None:
        out_shapes.append(HALF_UNIT)
    if inverse is not None:
        out_shapes.append(jax.ShapeDtypeStruct((2, WIDE, WIDE), jnp.bfloat16))

    def kernel(place_ref, bands_ref, gradient_ref, momentum_ref, forward_ref, *refs):
        extras, outs = refs[:n_extra], refs[n_extra : n_extra + len(out_shapes)]
        gradients, momenta, table, sems = refs[n_extra + len(out_shapes) :]
        core = place_ref[3]
        side = core if own else 1 - core
        columns = pl.ds(pl.multiple_of(side * HALF, LANES), HALF)
        pairs = [(forward_ref, table)]
        for i, unit in enumerate(units):
            layers = pl.ds(unit * UNIT, UNIT)
            pairs.append((gradient_ref.at[0, layers, :, columns], gradients.at[i]))
            pairs.append((momentum_ref.at[0, layers, :, columns], momenta.at[i]))
        at = 0 if received is None else 1
        if params is not None:
            pairs.append((extras[at].at[pl.ds(units[0] * UNIT, UNIT), :, columns], outs[count]))
            at += 1
        if inverse is not None:
            pairs.append((extras[at], outs[count + 1]))
        copies = [pltpu.make_async_copy(src, dst, sems.at[i]) for i, (src, dst) in enumerate(pairs)]
        for copy in copies:
            copy.start()
        copies[0].wait()
        for i, unit in enumerate(units):
            copies[1 + 2 * i].wait()
            copies[2 + 2 * i].wait()
            spectra = dot3(merged_rows(gradients[i], momenta[i]), table)
            layers = range(unit * UNIT, unit * UNIT + UNIT)
            for (layer, tile), values in pick_tiles(bands_ref, side, layers, spectra).items():
                where = (layer, slice(None), slice(tile * LANES, (tile + 1) * LANES))
                if received is not None:
                    values = values + extras[0][where].astype(jnp.float32)
                outs[i][where] = values.astype(jnp.bfloat16)
        for copy in copies[1 + 2 * count :]:
            copy.wait()

    extra_specs = ([] if received is None else [VMEM]) + [HBM] * (n_extra - (received is not None))
    return pl.pallas_call(
        kernel,
        out_shape=out_shapes,
        in_specs=[SMEM, VMEM, HBM, HBM, HBM] + extra_specs,
        out_specs=[VMEM] * len(out_shapes),
        scratch_shapes=[
            pltpu.VMEM((count, UNIT, ROWS_HERE, HALF), jnp.bfloat16),
            pltpu.VMEM((count, UNIT, ROWS_HERE, HALF), jnp.float32),
            pltpu.VMEM((2, WIDE, WIDE), jnp.bfloat16),
            pltpu.SemaphoreType.DMA((3 + 2 * count,)),
        ],
        compiler_params=pltpu.CompilerParams(vmem_limit_bytes=VMEM_LIMIT),
        cost_estimate=cost(6 * count * UNIT * ROWS_HERE * HALF * WIDE, count * 1500000),
    )(place, by_layer, gradient, momentum, forward, *extra)


def keep_rest(place, by_layer, gradient, momentum, forward, inverse, unit, before):
    def kernel(bands_ref, gradient_ref, momentum_ref, forward_ref, inverse_ref, *refs):
        out_ref, gradients, momenta, table, sems = refs[-5:]
        layers = pl.ds(unit * UNIT, UNIT)
        pairs = [(forward_ref, table)]
        for side in range(2):
            columns = pl.ds(side * HALF, HALF)
            pairs.append((gradient_ref.at[0, layers, :, columns], gradients.at[side]))
            pairs.append((momentum_ref.at[0, layers, :, columns], momenta.at[side]))
        copies = [pltpu.make_async_copy(src, dst, sems.at[i]) for i, (src, dst) in enumerate(pairs)]
        for copy in copies:
            copy.start()
        copies[0].wait()
        for side in range(2):
            copies[1 + 2 * side].wait()
            copies[2 + 2 * side].wait()
            merged = merged_rows(gradients[side], momenta[side])
            spectra = dot3(merged, table)
            tiles = pick_tiles(bands_ref, side, range(unit * UNIT, unit * UNIT + UNIT), spectra)
            wide = [
                jnp.concatenate([tiles[i, at], tiles[i, at + 1]], axis=1)
                for i in range(UNIT)
                for at in range(0, HALF // LANES, 2)
            ]
            kept = merged - dot3(jnp.concatenate(wide, axis=0), inverse_ref)
            for i in range(UNIT):
                for at in range(HALF // WIDE):
                    row = (i * (HALF // WIDE) + at) * ROWS_HERE
                    momenta[side, i, :, at * WIDE : (at + 1) * WIDE] = kept[row : row + ROWS_HERE]
            target = out_ref.at[0, layers, :, pl.ds(side * HALF, HALF)]
            copies.append(pltpu.make_async_copy(momenta.at[side], target, sems.at[5 + side]))
            copies[-1].start()
        copies[-2].wait()
        copies[-1].wait()

    operands = [by_layer, gradient, momentum, forward, inverse]
    specs = [VMEM, HBM, HBM, HBM, VMEM]
    aliases = {}
    if before is not None:
        aliases = {len(operands): 0}
        operands.append(before)
        specs.append(HBM)
    return pl.pallas_call(
        kernel,
        out_shape=jax.ShapeDtypeStruct(momentum.shape, jnp.float32),
        in_specs=specs,
        out_specs=HBM,
        scratch_shapes=[
            pltpu.VMEM((2, UNIT, ROWS_HERE, HALF), jnp.bfloat16),
            pltpu.VMEM((2, UNIT, ROWS_HERE, HALF), jnp.float32),
            pltpu.VMEM((2, WIDE, WIDE), jnp.bfloat16),
            pltpu.SemaphoreType.DMA((7,)),
        ],
        input_output_aliases=aliases,
        compiler_params=pltpu.CompilerParams(vmem_limit_bytes=VMEM_LIMIT),
        cost_estimate=cost(12 * UNIT * ROWS_HERE * WIDTH * WIDE, 3000000),
    )(*operands)


def decode(sums, params, inverse):
    def kernel(first, second, third, fourth, params_ref, inverse_ref, out_ref):
        total = first[...].astype(jnp.float32) + second[...].astype(jnp.float32)
        total += third[...].astype(jnp.float32) + fourth[...].astype(jnp.float32)
        total = total * (1.0 / REPS)
        restored = jnp.concatenate([stacked(total[i]) for i in range(UNIT)], axis=0)
        decoded = dot3(restored, inverse_ref)
        for i in range(UNIT):
            for at in range(HALF // WIDE):
                columns = slice(at * WIDE, (at + 1) * WIDE)
                row = (i * (HALF // WIDE) + at) * ROWS_HERE
                after = params_ref[i, :, columns].astype(jnp.float32) - step_size * decoded[row : row + ROWS_HERE]
                out_ref[i, :, columns] = after.astype(jnp.bfloat16)

    return pl.pallas_call(
        kernel,
        out_shape=HALF_UNIT,
        in_specs=[VMEM] * 6,
        out_specs=VMEM,
        compiler_params=pltpu.CompilerParams(vmem_limit_bytes=VMEM_LIMIT),
        cost_estimate=cost(6 * UNIT * ROWS_HERE * HALF * WIDE, 1500000),
    )(*sums, params, inverse)


def first_place(place_ref):
    return jnp.where(place_ref[3] == 0, place_ref[2], place_ref[1])


def second_place(place_ref):
    return jnp.where(place_ref[3] == 0, place_ref[1], place_ref[2])


def bring_together(place, blocks):
    def kernel(place_ref, *refs):
        here = first_place(place_ref)
        for (_, steps), block in zip(blocks, refs):
            refs[-1][:, lax.rem(here + (4 - steps), 4)] = block[...]

    return pl.pallas_call(
        kernel,
        out_shape=jax.ShapeDtypeStruct((UNIT, 4, ROWS_HERE, HALF), jnp.bfloat16),
        in_specs=[SMEM] + [VMEM] * len(blocks),
        out_specs=VMEM,
        compiler_params=pltpu.CompilerParams(vmem_limit_bytes=VMEM_LIMIT),
        cost_estimate=cost(0, 1800000),
    )(place, *[block for block, _ in blocks])


def write_blocks(place, whole, items):
    blocks = [item[0] for item in items]

    def kernel(place_ref, *refs):
        ins, out, sems = refs[: len(blocks)], refs[-2], refs[-1]
        y, x, core = place_ref[1], place_ref[2], place_ref[3]
        copies = []
        for block, (_, unit, steps, other) in zip(ins, items):
            side = core if other == 0 else 1 - core
            here = lax.rem(jnp.where(side == 0, y, x) + (4 - steps), 4)
            columns = pl.ds(pl.multiple_of(side * HALF, LANES), HALF)
            for i in range(4):
                rows = jnp.where(side == 0, 4 * here + i, 4 * i + here)
                target = out.at[pl.ds(unit * UNIT, UNIT), rows, :, columns]
                copies.append(pltpu.make_async_copy(block.at[:, i], target, sems.at[len(copies)]))
        for copy in copies:
            copy.start()
        for copy in copies:
            copy.wait()

    operands = [place] + blocks
    specs = [SMEM] + [VMEM] * len(blocks)
    aliases = {}
    if whole is not None:
        aliases = {len(operands): 0}
        operands.append(whole)
        specs.append(HBM)
    return pl.pallas_call(
        kernel,
        out_shape=jax.ShapeDtypeStruct((LAYERS, 16, ROWS_HERE, WIDTH), jnp.bfloat16),
        in_specs=specs,
        out_specs=HBM,
        scratch_shapes=[pltpu.SemaphoreType.DMA((4 * len(blocks),))],
        input_output_aliases=aliases,
        compiler_params=pltpu.CompilerParams(vmem_limit_bytes=VMEM_LIMIT),
        cost_estimate=cost(0, 2 * sum(b.size * 2 for b in blocks)),
    )(*operands)


def move(x, step):
    pairs = []
    for device in range(128):
        z, core, y, u = device // 32, device // 16 % 2, device // 4 % 4, device % 4
        z, core, y, u = step(z, core, y, u)
        pairs.append((device, (z % 4 * 2 + core) * 16 + y % 4 * 4 + u % 4))
    return lax.ppermute(x, ("rep", "fsdp"), pairs)


def swap(x):
    return move(x, lambda z, core, y, u: (z, 1 - core, y, u))


def ring_z(x):
    return move(x, lambda z, core, y, u: (z + 1 - 2 * core, core, y, u))


def along_first(x, by):
    return move(x, lambda z, core, y, u: (z, core, y, u + by) if core == 0 else (z, core, y + by, u))


def along_second(x, by):
    return move(x, lambda z, core, y, u: (z, core, y + by, u) if core == 0 else (z, core, y, u + by))


def spread(x, along, unit):
    ahead, behind = along(x, 1), along(x, -1)
    across = along(ahead, 1) if unit == 0 else along(behind, -1)
    return [(ahead, 1), (behind, 3), (across, 2)]


def shards(gradient, momentum, params, bands):
    rep, fsdp = lax.axis_index("rep"), lax.axis_index("fsdp")
    place = jnp.stack(
        [lax.shift_right_logical(rep, 1), lax.shift_right_logical(fsdp, 2), fsdp & 3, rep & 1]
    ).astype(jnp.int32)
    table = cosine_table()
    forward = split_table(np.kron(np.eye(WIDE // GROUP), table.T))
    inverse = split_table(np.kron(np.eye(WIDE // GROUP), table))
    blocks = HALF // GROUP
    by_layer = jnp.transpose(bands[0], (0, 3, 1, 2)).reshape(LAYERS, 2, ROWS_HERE, 2, blocks)
    by_layer = jnp.pad(jnp.transpose(by_layer, (0, 1, 3, 2, 4)), ((0, 0),) * 4 + ((0, LANES - blocks),))
    common = (place, by_layer, gradient, momentum, forward)

    theirs = pick(*common, range(UNITS), False)
    inverse_here = None
    updated, own = [], []
    for unit in range(UNITS):
        received = swap(theirs[unit])
        first = unit == 0
        picked = pick(*common, [unit], True, received, params, inverse if first else None)
        if first:
            inverse_here = picked[2]
        sums = [picked[0]]
        for _ in range(3):
            sums.append(ring_z(sums[-1]))
        updated.append(decode(sums, picked[1], inverse_here))
    near, far = [], []
    for unit in range(UNITS):
        block = updated[unit]
        block = bring_together(place, [(block, 0)] + spread(block, along_first, unit))
        ahead, behind, across = spread(block, along_second, unit)
        own.append((block, unit, 0))
        near += [(ahead[0], unit, 1), (behind[0], unit, 3)]
        far.append((across[0], unit, 2))

    new_momentum = None
    for unit in range(UNITS):
        new_momentum = keep_rest(*common, inverse_here, unit, new_momentum)

    whole = None
    for group in (own, near, far):
        items = [item + (0,) for item in group] + [(swap(item[0]),) + item[1:] + (1,) for item in group]
        whole = write_blocks(place, whole, items)
    return new_momentum, whole.reshape(LAYERS, 16 * ROWS_HERE, WIDTH)


def solution(mesh):
    in_specs = (
        P("rep", None, "fsdp", None),
        P("rep", None, "fsdp", None),
        P(None, "fsdp", None),
        P("rep", None, "fsdp", None, None),
    )
    out_specs = (P("rep", None, "fsdp", None), P())
    return jax.shard_map(shards, mesh=mesh, in_specs=in_specs, out_specs=out_specs, check_vma=False)
```

```python
import math

import jax
import jax.numpy as jnp
import numpy as np
from jax import lax
from jax.experimental import pallas as pl
from jax.experimental.pallas import tpu as pltpu
from jax.sharding import PartitionSpec as P

GROUP = 64
BANDS = 8
LAYERS = 4
ROWS_HERE = 8
WIDTH = 13824
HALF = WIDTH // 2
WIDE = 256
LANES = 128
REPS = 8
UNIT = 2
UNITS = LAYERS // UNIT

decay_rate = 0.9
step_size = 1.0
VMEM_LIMIT = 16 * 1024 * 1024
VMEM_FIRST = 16 * 1024 * 1024


def cosine_table():
    k = np.arange(GROUP, dtype=np.float64)
    n = np.arange(GROUP, dtype=np.float64)
    scale = np.where(k == 0, math.sqrt(1.0 / GROUP), math.sqrt(2.0 / GROUP))
    return scale[:, None] * np.cos(math.pi * (2.0 * n[None, :] + 1.0) * k[:, None] / (2.0 * GROUP))


def split_table(table):
    high = jnp.asarray(table, jnp.float32).astype(jnp.bfloat16)
    low = (jnp.asarray(table, jnp.float32) - high.astype(jnp.float32)).astype(jnp.bfloat16)
    return jnp.stack([high, low])


def dot3(x, table_ref):
    high = x.astype(jnp.bfloat16)
    low = (x - high.astype(jnp.float32)).astype(jnp.bfloat16)
    total = jnp.dot(high, table_ref[1], preferred_element_type=jnp.float32)
    total += jnp.dot(low, table_ref[0], preferred_element_type=jnp.float32)
    return total + jnp.dot(high, table_ref[0], preferred_element_type=jnp.float32)


def stacked(x):
    return jnp.concatenate([x[:, at : at + WIDE] for at in range(0, x.shape[1], WIDE)], axis=0)


def pick_tiles(bands_ref, side, layers, spectra):
    lane = lax.broadcasted_iota(jnp.int32, (ROWS_HERE, LANES), 1)
    upper = lax.shift_right_logical(lane, 6)
    band = lax.bitwise_and(lax.shift_right_logical(lane, 3), 7)
    tiles = {}
    for i, layer in enumerate(layers):
        first_bands = bands_ref[layer, 0, side]
        second_bands = bands_ref[layer, 1, side]
        for tile in range(HALF // LANES):
            index = upper + 2 * tile
            first = jnp.take_along_axis(first_bands, index, axis=1)
            second = jnp.take_along_axis(second_bands, index, axis=1)
            row = (i * (HALF // WIDE) + tile // 2) * ROWS_HERE
            column = (tile % 2) * LANES
            values = spectra[row : row + ROWS_HERE, column : column + LANES]
            tiles[i, tile] = jnp.where((first == band) | (second == band), values, 0.0)
    return tiles


def merged_rows(gradient, momentum):
    merged = decay_rate * momentum + gradient.astype(jnp.float32)
    return jnp.concatenate([stacked(merged[i]) for i in range(merged.shape[0])], axis=0)


HBM = pl.BlockSpec(memory_space=pl.ANY)
VMEM = pl.BlockSpec(memory_space=pltpu.VMEM)
SMEM = pl.BlockSpec(memory_space=pltpu.SMEM)
HALF_UNIT = jax.ShapeDtypeStruct((UNIT, ROWS_HERE, HALF), jnp.bfloat16)
HALF_LAYERS = jax.ShapeDtypeStruct((LAYERS, ROWS_HERE, HALF), jnp.bfloat16)
HALF_MOMENTUM = jax.ShapeDtypeStruct((LAYERS, ROWS_HERE, HALF), jnp.float32)
TABLE = jax.ShapeDtypeStruct((2, WIDE, WIDE), jnp.bfloat16)
TOKEN = jax.ShapeDtypeStruct((8, 128), jnp.float32)


def cost(flops, size):
    return pl.CostEstimate(flops=flops, bytes_accessed=size, transcendentals=0)


def store_picked(bands_ref, side, unit, spectra, out_ref):
    layers = range(unit * UNIT, unit * UNIT + UNIT)
    for (layer, tile), values in pick_tiles(bands_ref, side, layers, spectra).items():
        out_ref[unit * UNIT + layer, :, tile * LANES : (tile + 1) * LANES] = values.astype(jnp.bfloat16)


def pick_theirs(place, by_layer, gradient, momentum, params, forward, inverse):
    out_shapes = [HALF_LAYERS, HALF_LAYERS, HALF_MOMENTUM, HALF_LAYERS, TABLE, TABLE]

    def kernel(place_ref, bands_ref, gradient_ref, momentum_ref, params_ref, forward_ref, inverse_ref, *refs):
        picked, own_gradient, own_momentum, own_params, table, back_table, gradients, momenta, sems = refs
        core = place_ref[3]
        own = pl.ds(pl.multiple_of(core * HALF, LANES), HALF)
        theirs = pl.ds(pl.multiple_of((1 - core) * HALF, LANES), HALF)
        pairs = [(forward_ref, table)]
        for unit in range(UNITS):
            layers = pl.ds(unit * UNIT, UNIT)
            pairs.append((gradient_ref.at[0, layers, :, theirs], gradients.at[layers]))
            pairs.append((momentum_ref.at[0, layers, :, theirs], momenta.at[layers]))
        pairs.append((gradient_ref.at[0, :, :, own], own_gradient))
        pairs.append((momentum_ref.at[0, :, :, own], own_momentum))
        pairs.append((params_ref.at[:, :, own], own_params))
        pairs.append((inverse_ref, back_table))
        copies = [pltpu.make_async_copy(src, dst, sems.at[i]) for i, (src, dst) in enumerate(pairs)]
        for copy in copies:
            copy.start()
        copies[0].wait()
        for unit in range(UNITS):
            copies[1 + 2 * unit].wait()
            copies[2 + 2 * unit].wait()
            layers = slice(unit * UNIT, unit * UNIT + UNIT)
            spectra = dot3(merged_rows(gradients[layers], momenta[layers]), table)
            store_picked(bands_ref, 1 - core, unit, spectra, picked)
        for copy in copies[1 + 2 * UNITS :]:
            copy.wait()

    return pl.pallas_call(
        kernel,
        out_shape=out_shapes,
        in_specs=[SMEM, VMEM] + [HBM] * 5,
        out_specs=[VMEM] * len(out_shapes),
        scratch_shapes=[
            pltpu.VMEM((LAYERS, ROWS_HERE, HALF), jnp.bfloat16),
            pltpu.VMEM((LAYERS, ROWS_HERE, HALF), jnp.float32),
            pltpu.SemaphoreType.DMA((5 + 2 * UNITS,)),
        ],
        compiler_params=pltpu.CompilerParams(vmem_limit_bytes=VMEM_FIRST),
        cost_estimate=cost(6 * LAYERS * ROWS_HERE * HALF * WIDE, 6000000),
    )(place, by_layer, gradient, momentum, params, forward, inverse)


def pick_own(place, by_layer, gradient, momentum, forward):
    def kernel(place_ref, bands_ref, gradient_ref, momentum_ref, table_ref, picked):
        for unit in range(UNITS):
            layers = slice(unit * UNIT, unit * UNIT + UNIT)
            spectra = dot3(merged_rows(gradient_ref[layers], momentum_ref[layers]), table_ref)
            store_picked(bands_ref, place_ref[3], unit, spectra, picked)

    return pl.pallas_call(
        kernel,
        out_shape=HALF_LAYERS,
        in_specs=[SMEM] + [VMEM] * 4,
        out_specs=VMEM,
        compiler_params=pltpu.CompilerParams(vmem_limit_bytes=VMEM_LIMIT),
        cost_estimate=cost(6 * LAYERS * ROWS_HERE * HALF * WIDE, 2000000),
    )(place, by_layer, gradient, momentum, forward)


def pair_sum(mine, received, tokens=()):
    def kernel(mine_ref, received_ref, *refs):
        total = mine_ref[...].astype(jnp.float32) + received_ref[...].astype(jnp.float32)
        refs[-1][...] = total.astype(jnp.bfloat16)

    return pl.pallas_call(
        kernel,
        out_shape=HALF_LAYERS,
        in_specs=[VMEM] * (2 + len(tokens)),
        out_specs=VMEM,
        compiler_params=pltpu.CompilerParams(vmem_limit_bytes=VMEM_LIMIT),
        cost_estimate=cost(0, 1400000),
    )(mine, received, *tokens)


def keep_rest(place, by_layer, gradient, momentum, forward, inverse, unit, before):
    def kernel(bands_ref, gradient_ref, momentum_ref, forward_ref, inverse_ref, *refs):
        out_ref, token_ref, gradients, momenta, table, sems = refs[-6:]
        token_ref[...] = jnp.zeros_like(token_ref)
        layers = pl.ds(unit * UNIT, UNIT)
        pairs = [(forward_ref, table)]
        for side in range(2):
            columns = pl.ds(side * HALF, HALF)
            pairs.append((gradient_ref.at[0, layers, :, columns], gradients.at[side]))
            pairs.append((momentum_ref.at[0, layers, :, columns], momenta.at[side]))
        copies = [pltpu.make_async_copy(src, dst, sems.at[i]) for i, (src, dst) in enumerate(pairs)]
        for copy in copies:
            copy.start()
        copies[0].wait()
        for side in range(2):
            copies[1 + 2 * side].wait()
            copies[2 + 2 * side].wait()
            merged = merged_rows(gradients[side], momenta[side])
            spectra = dot3(merged, table)
            tiles = pick_tiles(bands_ref, side, range(unit * UNIT, unit * UNIT + UNIT), spectra)
            wide = [
                jnp.concatenate([tiles[i, at], tiles[i, at + 1]], axis=1)
                for i in range(UNIT)
                for at in range(0, HALF // LANES, 2)
            ]
            kept = merged - dot3(jnp.concatenate(wide, axis=0), inverse_ref)
            for i in range(UNIT):
                for at in range(HALF // WIDE):
                    row = (i * (HALF // WIDE) + at) * ROWS_HERE
                    momenta[side, i, :, at * WIDE : (at + 1) * WIDE] = kept[row : row + ROWS_HERE]
            target = out_ref.at[0, layers, :, pl.ds(side * HALF, HALF)]
            copies.append(pltpu.make_async_copy(momenta.at[side], target, sems.at[5 + side]))
            copies[-1].start()
        copies[-2].wait()
        copies[-1].wait()

    operands = [by_layer, gradient, momentum, forward, inverse]
    specs = [VMEM, HBM, HBM, HBM, VMEM]
    aliases = {}
    if before is not None:
        aliases = {len(operands): 0}
        operands.append(before)
        specs.append(HBM)
    return pl.pallas_call(
        kernel,
        out_shape=[jax.ShapeDtypeStruct(momentum.shape, jnp.float32), TOKEN],
        in_specs=specs,
        out_specs=[HBM, VMEM],
        scratch_shapes=[
            pltpu.VMEM((2, UNIT, ROWS_HERE, HALF), jnp.bfloat16),
            pltpu.VMEM((2, UNIT, ROWS_HERE, HALF), jnp.float32),
            pltpu.VMEM((2, WIDE, WIDE), jnp.bfloat16),
            pltpu.SemaphoreType.DMA((7,)),
        ],
        input_output_aliases=aliases,
        compiler_params=pltpu.CompilerParams(vmem_limit_bytes=VMEM_LIMIT),
        cost_estimate=cost(12 * UNIT * ROWS_HERE * WIDTH * WIDE, 3000000),
    )(*operands)


def decode(mine, received, params, inverse, tokens):
    def kernel(mine_ref, received_ref, params_ref, inverse_ref, *refs):
        for layer in range(LAYERS):
            total = mine_ref[layer].astype(jnp.float32) + received_ref[layer].astype(jnp.float32)
            restored = stacked(total * (1.0 / REPS))
            restored = jnp.concatenate([restored, jnp.zeros((ROWS_HERE, WIDE), jnp.float32)], axis=0)
            decoded = dot3(restored, inverse_ref)
            for at in range(HALF // WIDE):
                columns = slice(at * WIDE, (at + 1) * WIDE)
                change = step_size * decoded[at * ROWS_HERE : (at + 1) * ROWS_HERE]
                updated = params_ref[layer, :, columns].astype(jnp.float32) - change
                refs[-1][layer, :, columns] = updated.astype(jnp.bfloat16)

    return pl.pallas_call(
        kernel,
        out_shape=HALF_LAYERS,
        in_specs=[VMEM] * (4 + len(tokens)),
        out_specs=VMEM,
        compiler_params=pltpu.CompilerParams(vmem_limit_bytes=VMEM_LIMIT),
        cost_estimate=cost(6 * LAYERS * ROWS_HERE * HALF * WIDE, 3000000),
    )(mine, received, params, inverse, *tokens)


def first_place(place_ref):
    return jnp.where(place_ref[3] == 0, place_ref[2], place_ref[1])


def second_place(place_ref):
    return jnp.where(place_ref[3] == 0, place_ref[1], place_ref[2])


def bring_together(place, blocks):
    def kernel(place_ref, *refs):
        here = first_place(place_ref)
        for (_, steps), block in zip(blocks, refs):
            for unit in range(UNITS):
                source = lax.rem(here + (4 - steps), 4)
                refs[len(blocks) + unit][:, source] = block[unit * UNIT : (unit + 1) * UNIT]

    return pl.pallas_call(
        kernel,
        out_shape=[jax.ShapeDtypeStruct((UNIT, 4, ROWS_HERE, HALF), jnp.bfloat16)] * UNITS,
        in_specs=[SMEM] + [VMEM] * len(blocks),
        out_specs=[VMEM] * UNITS,
        compiler_params=pltpu.CompilerParams(vmem_limit_bytes=VMEM_LIMIT),
        cost_estimate=cost(0, 3600000),
    )(place, *[block for block, _ in blocks])


def write_blocks(place, whole, items):
    blocks = [item[0] for item in items]

    def kernel(place_ref, *refs):
        ins, (out, token_ref, sems) = refs[: len(blocks)], refs[-3:]
        token_ref[...] = jnp.zeros_like(token_ref)
        y, x, core = place_ref[1], place_ref[2], place_ref[3]
        copies = []
        for block, (_, unit, steps, other) in zip(ins, items):
            side = core if other == 0 else 1 - core
            here = lax.rem(jnp.where(side == 0, y, x) + (4 - steps), 4)
            columns = pl.ds(pl.multiple_of(side * HALF, LANES), HALF)
            for i in range(4):
                rows = jnp.where(side == 0, 4 * here + i, 4 * i + here)
                for layer in range(UNIT):
                    target = out.at[unit * UNIT + layer, rows, :, columns]
                    copies.append(pltpu.make_async_copy(block.at[layer, i], target, sems.at[len(copies)]))
        for copy in copies:
            copy.start()
        for copy in copies:
            copy.wait()

    operands = [place] + blocks
    specs = [SMEM] + [VMEM] * len(blocks)
    aliases = {}
    if whole is not None:
        aliases = {len(operands): 0}
        operands.append(whole)
        specs.append(HBM)
    return pl.pallas_call(
        kernel,
        out_shape=[jax.ShapeDtypeStruct((LAYERS, 16, ROWS_HERE, WIDTH), jnp.bfloat16), TOKEN],
        in_specs=specs,
        out_specs=[HBM, VMEM],
        scratch_shapes=[pltpu.SemaphoreType.DMA((4 * UNIT * len(blocks),))],
        input_output_aliases=aliases,
        compiler_params=pltpu.CompilerParams(vmem_limit_bytes=VMEM_LIMIT),
        cost_estimate=cost(0, 2 * sum(b.size * 2 for b in blocks)),
    )(*operands)


def move(x, step):
    pairs = []
    for device in range(128):
        z, core, y, u = device // 32, device // 16 % 2, device // 4 % 4, device % 4
        z, core, y, u = step(z, core, y, u)
        pairs.append((device, (z % 4 * 2 + core) * 16 + y % 4 * 4 + u % 4))
    return lax.ppermute(x, ("rep", "fsdp"), pairs)


def swap(x):
    return move(x, lambda z, core, y, u: (z, 1 - core, y, u))


def along_first(x, by):
    return move(x, lambda z, core, y, u: (z, core, y, u + by) if core == 0 else (z, core, y + by, u))


def along_second(x, by):
    return move(x, lambda z, core, y, u: (z, core, y + by, u) if core == 0 else (z, core, y, u + by))


def after(x, *tokens):
    def kernel(x_ref, *refs):
        pass

    return pl.pallas_call(
        kernel,
        out_shape=jax.ShapeDtypeStruct(x.shape, x.dtype),
        in_specs=[VMEM] * (1 + len(tokens)),
        out_specs=VMEM,
        input_output_aliases={0: 0},
        compiler_params=pltpu.CompilerParams(vmem_limit_bytes=VMEM_LIMIT),
        cost_estimate=cost(0, 4096),
    )(x, *tokens)


def spread(x, along, unit, tokens=()):
    ahead, behind = along(x, 1), along(x, -1)
    if tokens and unit == 0:
        ahead = after(ahead, *tokens)
    elif tokens:
        behind = after(behind, *tokens)
    across = along(ahead, 1) if unit == 0 else along(behind, -1)
    return [(ahead, 1), (behind, 3), (across, 2)]


def exchange_z(x, step):
    return move(x, lambda z, core, y, u: (z ^ 1 if core == step else 3 - z, core, y, u))


def shards(gradient, momentum, params, bands):
    rep, fsdp = lax.axis_index("rep"), lax.axis_index("fsdp")
    place = jnp.stack(
        [lax.shift_right_logical(rep, 1), lax.shift_right_logical(fsdp, 2), fsdp & 3, rep & 1]
    ).astype(jnp.int32)
    table = cosine_table()
    forward = split_table(np.kron(np.eye(WIDE // GROUP), table.T))
    inverse = split_table(np.kron(np.eye(WIDE // GROUP), table))
    blocks = HALF // GROUP
    by_layer = jnp.transpose(bands[0], (0, 3, 1, 2)).reshape(LAYERS, 2, ROWS_HERE, 2, blocks)
    by_layer = jnp.pad(jnp.transpose(by_layer, (0, 1, 3, 2, 4)), ((0, 0),) * 4 + ((0, LANES - blocks),))

    gradient, momentum, params, forward, inverse = (
        pltpu.with_memory_space_constraint(x, pltpu.HBM) for x in (gradient, momentum, params, forward, inverse)
    )
    theirs, own_gradient, own_momentum, own_params, forward_here, inverse_here = pick_theirs(
        place, by_layer, gradient, momentum, params, forward, inverse
    )
    received = swap(theirs)
    mine = pick_own(place, by_layer, own_gradient, own_momentum, forward_here)
    new_momentum, tokens = None, []
    for unit in range(UNITS):
        new_momentum, token = keep_rest(place, by_layer, gradient, momentum, forward_here, inverse_here, unit, new_momentum)
        tokens.append(token)
    chip = pair_sum(mine, received)
    two_chips = pair_sum(chip, exchange_z(chip, 0), tokens[:1])
    block = decode(two_chips, exchange_z(two_chips, 1), own_params, inverse_here, tokens[1:])
    own = bring_together(place, [(block, 0)] + spread(block, along_first, 0))

    items = []
    for unit, block in enumerate(own):
        items += [(block, unit, 0, 0), (swap(block), unit, 0, 1)]
    whole, token = write_blocks(place, None, items)
    far, tokens = [], [token]
    for unit, block in enumerate(own):
        ahead, behind, across = spread(block, along_second, unit, tokens)
        near = []
        for moved, steps in (ahead, behind):
            near += [(moved, unit, steps, 0), (swap(moved), unit, steps, 1)]
        whole, token = write_blocks(place, whole, near)
        tokens.append(token)
        far.append(across[0])
    far[1] = after(far[1], *tokens)
    for unit, block in enumerate(far):
        whole, token = write_blocks(place, whole, [(block, unit, 2, 0), (swap(block), unit, 2, 1)])
    return new_momentum, whole.reshape(LAYERS, 16 * ROWS_HERE, WIDTH)


def solution(mesh):
    in_specs = (
        P("rep", None, "fsdp", None),
        P("rep", None, "fsdp", None),
        P(None, "fsdp", None),
        P("rep", None, "fsdp", None, None),
    )
    out_specs = (P("rep", None, "fsdp", None), P())
    return jax.shard_map(shards, mesh=mesh, in_specs=in_specs, out_specs=out_specs, check_vma=False)
```

```python
import math

import jax
import jax.numpy as jnp
import numpy as np
from jax import lax
from jax.experimental import pallas as pl
from jax.experimental.pallas import tpu as pltpu
from jax.sharding import PartitionSpec as P

GROUP = 64
BANDS = 8
LAYERS = 4
ROWS_HERE = 8
WIDTH = 13824
HALF = WIDTH // 2
WIDE = 256
LANES = 128
REPS = 8
UNIT = 2
UNITS = LAYERS // UNIT

decay_rate = 0.9
step_size = 1.0
VMEM_LIMIT = 16 * 1024 * 1024
VMEM_FIRST = 16 * 1024 * 1024


def cosine_table():
    k = np.arange(GROUP, dtype=np.float64)
    n = np.arange(GROUP, dtype=np.float64)
    scale = np.where(k == 0, math.sqrt(1.0 / GROUP), math.sqrt(2.0 / GROUP))
    return scale[:, None] * np.cos(math.pi * (2.0 * n[None, :] + 1.0) * k[:, None] / (2.0 * GROUP))


def split_table(table):
    high = jnp.asarray(table, jnp.float32).astype(jnp.bfloat16)
    low = (jnp.asarray(table, jnp.float32) - high.astype(jnp.float32)).astype(jnp.bfloat16)
    return jnp.stack([high, low])


def dot3(x, table_ref):
    high = x.astype(jnp.bfloat16)
    low = (x - high.astype(jnp.float32)).astype(jnp.bfloat16)
    total = jnp.dot(high, table_ref[1], preferred_element_type=jnp.float32)
    total += jnp.dot(low, table_ref[0], preferred_element_type=jnp.float32)
    return total + jnp.dot(high, table_ref[0], preferred_element_type=jnp.float32)


def stacked(x):
    return jnp.concatenate([x[:, at : at + WIDE] for at in range(0, x.shape[1], WIDE)], axis=0)


def pick_tiles(bands_ref, side, layers, spectra):
    lane = lax.broadcasted_iota(jnp.int32, (ROWS_HERE, LANES), 1)
    upper = lax.shift_right_logical(lane, 6)
    band = lax.bitwise_and(lax.shift_right_logical(lane, 3), 7)
    tiles = {}
    for i, layer in enumerate(layers):
        first_bands = bands_ref[layer, 0, side]
        second_bands = bands_ref[layer, 1, side]
        for tile in range(HALF // LANES):
            index = upper + 2 * tile
            first = jnp.take_along_axis(first_bands, index, axis=1)
            second = jnp.take_along_axis(second_bands, index, axis=1)
            row = (i * (HALF // WIDE) + tile // 2) * ROWS_HERE
            column = (tile % 2) * LANES
            values = spectra[row : row + ROWS_HERE, column : column + LANES]
            tiles[i, tile] = jnp.where((first == band) | (second == band), values, 0.0)
    return tiles


def merged_rows(gradient, momentum):
    merged = decay_rate * momentum + gradient.astype(jnp.float32)
    return jnp.concatenate([stacked(merged[i]) for i in range(merged.shape[0])], axis=0)


HBM = pl.BlockSpec(memory_space=pl.ANY)
VMEM = pl.BlockSpec(memory_space=pltpu.VMEM)
SMEM = pl.BlockSpec(memory_space=pltpu.SMEM)
HALF_UNIT = jax.ShapeDtypeStruct((UNIT, ROWS_HERE, HALF), jnp.bfloat16)
HALF_LAYERS = jax.ShapeDtypeStruct((LAYERS, ROWS_HERE, HALF), jnp.bfloat16)
HALF_MOMENTUM = jax.ShapeDtypeStruct((LAYERS, ROWS_HERE, HALF), jnp.float32)
TABLE = jax.ShapeDtypeStruct((2, WIDE, WIDE), jnp.bfloat16)
TOKEN = jax.ShapeDtypeStruct((8, 128), jnp.float32)


def cost(flops, size):
    return pl.CostEstimate(flops=flops, bytes_accessed=size, transcendentals=0)


def store_picked(bands_ref, side, unit, spectra, out_ref):
    layers = range(unit * UNIT, unit * UNIT + UNIT)
    for (layer, tile), values in pick_tiles(bands_ref, side, layers, spectra).items():
        out_ref[unit * UNIT + layer, :, tile * LANES : (tile + 1) * LANES] = values.astype(jnp.bfloat16)


def pick_theirs(place, by_layer, gradient, momentum, params, forward, inverse):
    out_shapes = [HALF_LAYERS, HALF_LAYERS, HALF_MOMENTUM, HALF_LAYERS, TABLE, TABLE]

    def kernel(place_ref, bands_ref, gradient_ref, momentum_ref, params_ref, forward_ref, inverse_ref, *refs):
        picked, own_gradient, own_momentum, own_params, table, back_table, gradients, momenta, sems = refs
        core = place_ref[3]
        own = pl.ds(pl.multiple_of(core * HALF, LANES), HALF)
        theirs = pl.ds(pl.multiple_of((1 - core) * HALF, LANES), HALF)
        pairs = [(forward_ref, table)]
        for unit in range(UNITS):
            layers = pl.ds(unit * UNIT, UNIT)
            pairs.append((gradient_ref.at[0, layers, :, theirs], gradients.at[layers]))
            pairs.append((momentum_ref.at[0, layers, :, theirs], momenta.at[layers]))
        pairs.append((gradient_ref.at[0, :, :, own], own_gradient))
        pairs.append((momentum_ref.at[0, :, :, own], own_momentum))
        pairs.append((params_ref.at[:, :, own], own_params))
        pairs.append((inverse_ref, back_table))
        copies = [pltpu.make_async_copy(src, dst, sems.at[i]) for i, (src, dst) in enumerate(pairs)]
        for copy in copies:
            copy.start()
        copies[0].wait()
        for unit in range(UNITS):
            copies[1 + 2 * unit].wait()
            copies[2 + 2 * unit].wait()
            layers = slice(unit * UNIT, unit * UNIT + UNIT)
            spectra = dot3(merged_rows(gradients[layers], momenta[layers]), table)
            store_picked(bands_ref, 1 - core, unit, spectra, picked)
        for copy in copies[1 + 2 * UNITS :]:
            copy.wait()

    return pl.pallas_call(
        kernel,
        out_shape=out_shapes,
        in_specs=[SMEM, VMEM] + [HBM] * 5,
        out_specs=[VMEM] * len(out_shapes),
        scratch_shapes=[
            pltpu.VMEM((LAYERS, ROWS_HERE, HALF), jnp.bfloat16),
            pltpu.VMEM((LAYERS, ROWS_HERE, HALF), jnp.float32),
            pltpu.SemaphoreType.DMA((5 + 2 * UNITS,)),
        ],
        compiler_params=pltpu.CompilerParams(vmem_limit_bytes=VMEM_FIRST),
        cost_estimate=cost(6 * LAYERS * ROWS_HERE * HALF * WIDE, 6000000),
    )(place, by_layer, gradient, momentum, params, forward, inverse)


def pick_own(place, by_layer, gradient, momentum, forward):
    def kernel(place_ref, bands_ref, gradient_ref, momentum_ref, table_ref, picked):
        for unit in range(UNITS):
            layers = slice(unit * UNIT, unit * UNIT + UNIT)
            spectra = dot3(merged_rows(gradient_ref[layers], momentum_ref[layers]), table_ref)
            store_picked(bands_ref, place_ref[3], unit, spectra, picked)

    return pl.pallas_call(
        kernel,
        out_shape=HALF_LAYERS,
        in_specs=[SMEM] + [VMEM] * 4,
        out_specs=VMEM,
        compiler_params=pltpu.CompilerParams(vmem_limit_bytes=VMEM_LIMIT),
        cost_estimate=cost(6 * LAYERS * ROWS_HERE * HALF * WIDE, 2000000),
    )(place, by_layer, gradient, momentum, forward)


def chip_sums(mine, received):
    def kernel(mine_ref, received_ref, *outs):
        for unit, out_ref in enumerate(outs):
            layers = slice(unit * UNIT, (unit + 1) * UNIT)
            total = mine_ref[layers].astype(jnp.float32) + received_ref[layers].astype(jnp.float32)
            out_ref[...] = total.astype(jnp.bfloat16)

    return pl.pallas_call(
        kernel,
        out_shape=[HALF_UNIT] * UNITS,
        in_specs=[VMEM] * 2,
        out_specs=[VMEM] * UNITS,
        compiler_params=pltpu.CompilerParams(vmem_limit_bytes=VMEM_LIMIT),
        cost_estimate=cost(0, 1400000),
    )(mine, received)


def pair_sum(mine, received, tokens=()):
    def kernel(mine_ref, received_ref, *refs):
        total = mine_ref[...].astype(jnp.float32) + received_ref[...].astype(jnp.float32)
        refs[-1][...] = total.astype(jnp.bfloat16)

    return pl.pallas_call(
        kernel,
        out_shape=HALF_UNIT,
        in_specs=[VMEM] * (2 + len(tokens)),
        out_specs=VMEM,
        compiler_params=pltpu.CompilerParams(vmem_limit_bytes=VMEM_LIMIT),
        cost_estimate=cost(0, 700000),
    )(mine, received, *tokens)


def keep_rest(place, by_layer, gradient, momentum, forward, inverse, unit, before, tokens=()):
    def kernel(bands_ref, gradient_ref, momentum_ref, forward_ref, inverse_ref, *refs):
        out_ref, token_ref, gradients, momenta, table, sems = refs[-6:]
        token_ref[...] = jnp.zeros_like(token_ref)
        layers = pl.ds(unit * UNIT, UNIT)
        pairs = [(forward_ref, table)]
        for side in range(2):
            columns = pl.ds(side * HALF, HALF)
            pairs.append((gradient_ref.at[0, layers, :, columns], gradients.at[side]))
            pairs.append((momentum_ref.at[0, layers, :, columns], momenta.at[side]))
        copies = [pltpu.make_async_copy(src, dst, sems.at[i]) for i, (src, dst) in enumerate(pairs)]
        for copy in copies:
            copy.start()
        copies[0].wait()
        for side in range(2):
            copies[1 + 2 * side].wait()
            copies[2 + 2 * side].wait()
            merged = merged_rows(gradients[side], momenta[side])
            spectra = dot3(merged, table)
            tiles = pick_tiles(bands_ref, side, range(unit * UNIT, unit * UNIT + UNIT), spectra)
            wide = [
                jnp.concatenate([tiles[i, at], tiles[i, at + 1]], axis=1)
                for i in range(UNIT)
                for at in range(0, HALF // LANES, 2)
            ]
            kept = merged - dot3(jnp.concatenate(wide, axis=0), inverse_ref)
            for i in range(UNIT):
                for at in range(HALF // WIDE):
                    row = (i * (HALF // WIDE) + at) * ROWS_HERE
                    momenta[side, i, :, at * WIDE : (at + 1) * WIDE] = kept[row : row + ROWS_HERE]
            target = out_ref.at[0, layers, :, pl.ds(side * HALF, HALF)]
            copies.append(pltpu.make_async_copy(momenta.at[side], target, sems.at[5 + side]))
            copies[-1].start()
        copies[-2].wait()
        copies[-1].wait()

    operands = [by_layer, gradient, momentum, forward, inverse, *tokens]
    specs = [VMEM, HBM, HBM, HBM, VMEM] + [VMEM] * len(tokens)
    aliases = {}
    if before is not None:
        aliases = {len(operands): 0}
        operands.append(before)
        specs.append(HBM)
    return pl.pallas_call(
        kernel,
        out_shape=[jax.ShapeDtypeStruct(momentum.shape, jnp.float32), TOKEN],
        in_specs=specs,
        out_specs=[HBM, VMEM],
        scratch_shapes=[
            pltpu.VMEM((2, UNIT, ROWS_HERE, HALF), jnp.bfloat16),
            pltpu.VMEM((2, UNIT, ROWS_HERE, HALF), jnp.float32),
            pltpu.VMEM((2, WIDE, WIDE), jnp.bfloat16),
            pltpu.SemaphoreType.DMA((7,)),
        ],
        input_output_aliases=aliases,
        compiler_params=pltpu.CompilerParams(vmem_limit_bytes=VMEM_LIMIT),
        cost_estimate=cost(12 * UNIT * ROWS_HERE * WIDTH * WIDE, 3000000),
    )(*operands)


def decode(mine, received, params, inverse, unit, tokens=()):
    def kernel(mine_ref, received_ref, params_ref, inverse_ref, *refs):
        total = mine_ref[...].astype(jnp.float32) + received_ref[...].astype(jnp.float32)
        total = total * (1.0 / REPS)
        restored = jnp.concatenate([stacked(total[i]) for i in range(UNIT)], axis=0)
        decoded = dot3(restored, inverse_ref)
        for i in range(UNIT):
            for at in range(HALF // WIDE):
                columns = slice(at * WIDE, (at + 1) * WIDE)
                row = (i * (HALF // WIDE) + at) * ROWS_HERE
                change = step_size * decoded[row : row + ROWS_HERE]
                updated = params_ref[unit * UNIT + i, :, columns].astype(jnp.float32) - change
                refs[-1][i, :, columns] = updated.astype(jnp.bfloat16)

    return pl.pallas_call(
        kernel,
        out_shape=HALF_UNIT,
        in_specs=[VMEM] * (4 + len(tokens)),
        out_specs=VMEM,
        compiler_params=pltpu.CompilerParams(vmem_limit_bytes=VMEM_LIMIT),
        cost_estimate=cost(6 * UNIT * ROWS_HERE * HALF * WIDE, 1500000),
    )(mine, received, params, inverse, *tokens)


def first_place(place_ref):
    return jnp.where(place_ref[3] == 0, place_ref[2], place_ref[1])


def second_place(place_ref):
    return jnp.where(place_ref[3] == 0, place_ref[1], place_ref[2])


def bring_together(place, units):
    blocks = [block for unit in units for block, _ in unit]

    def kernel(place_ref, *refs):
        here = first_place(place_ref)
        ins = iter(refs)
        for at, unit in enumerate(units):
            for _, steps in unit:
                refs[-1][at * UNIT : (at + 1) * UNIT, lax.rem(here + (4 - steps), 4)] = next(ins)[...]

    return pl.pallas_call(
        kernel,
        out_shape=jax.ShapeDtypeStruct((LAYERS, 4, ROWS_HERE, HALF), jnp.bfloat16),
        in_specs=[SMEM] + [VMEM] * len(blocks),
        out_specs=VMEM,
        compiler_params=pltpu.CompilerParams(vmem_limit_bytes=VMEM_LIMIT),
        cost_estimate=cost(0, 3600000),
    )(place, *blocks)


def write_blocks(place, whole, items):
    blocks = [item[0] for item in items]

    def kernel(place_ref, *refs):
        ins, (out, token_ref, sems) = refs[: len(blocks)], refs[-3:]
        token_ref[...] = jnp.zeros_like(token_ref)
        y, x, core = place_ref[1], place_ref[2], place_ref[3]
        copies = []
        for block, (_, first_layer, steps, other) in zip(ins, items):
            side = core if other == 0 else 1 - core
            columns = pl.ds(pl.multiple_of(side * HALF, LANES), HALF)
            here = lax.rem(jnp.where(side == 0, y, x) + (4 - steps), 4)
            for i in range(4):
                rows = jnp.where(side == 0, 4 * here + i, 4 * i + here)
                for layer in range(block.shape[0]):
                    target = out.at[first_layer + layer, rows, :, columns]
                    copies.append(pltpu.make_async_copy(block.at[layer, i], target, sems.at[len(copies)]))
        for copy in copies:
            copy.start()
        for copy in copies:
            copy.wait()

    operands = [place] + blocks
    specs = [SMEM] + [VMEM] * len(blocks)
    aliases = {}
    if whole is not None:
        aliases = {len(operands): 0}
        operands.append(whole)
        specs.append(HBM)
    return pl.pallas_call(
        kernel,
        out_shape=[jax.ShapeDtypeStruct((LAYERS, 16, ROWS_HERE, WIDTH), jnp.bfloat16), TOKEN],
        in_specs=specs,
        out_specs=[HBM, VMEM],
        scratch_shapes=[pltpu.SemaphoreType.DMA((4 * sum(block.shape[0] for block in blocks),))],
        input_output_aliases=aliases,
        compiler_params=pltpu.CompilerParams(vmem_limit_bytes=VMEM_LIMIT),
        cost_estimate=cost(0, 2 * sum(b.size * 2 for b in blocks)),
    )(*operands)


def move(x, step):
    pairs = []
    for device in range(128):
        z, core, y, u = device // 32, device // 16 % 2, device // 4 % 4, device % 4
        z, core, y, u = step(z, core, y, u)
        pairs.append((device, (z % 4 * 2 + core) * 16 + y % 4 * 4 + u % 4))
    return lax.ppermute(x, ("rep", "fsdp"), pairs)


def swap(x):
    return move(x, lambda z, core, y, u: (z, 1 - core, y, u))


def along_first(x, by):
    return move(x, lambda z, core, y, u: (z, core, y, u + by) if core == 0 else (z, core, y + by, u))


def along_second(x, by):
    return move(x, lambda z, core, y, u: (z, core, y + by, u) if core == 0 else (z, core, y, u + by))


def after(x, *tokens):
    def kernel(x_ref, *refs):
        pass

    return pl.pallas_call(
        kernel,
        out_shape=jax.ShapeDtypeStruct(x.shape, x.dtype),
        in_specs=[VMEM] * (1 + len(tokens)),
        out_specs=VMEM,
        input_output_aliases={0: 0},
        compiler_params=pltpu.CompilerParams(vmem_limit_bytes=VMEM_LIMIT),
        cost_estimate=cost(0, 4096),
    )(x, *tokens)


def copied(x, token):
    def kernel(x_ref, token_ref, out_ref):
        out_ref[...] = x_ref[...]

    return pl.pallas_call(
        kernel,
        out_shape=jax.ShapeDtypeStruct(x.shape, x.dtype),
        in_specs=[VMEM] * 2,
        out_specs=VMEM,
        compiler_params=pltpu.CompilerParams(vmem_limit_bytes=VMEM_LIMIT),
        cost_estimate=cost(0, 2 * x.size * 2),
    )(x, token)


def part(x, unit):
    def kernel(x_ref, *refs):
        refs[-1][...] = x_ref[unit * UNIT : (unit + 1) * UNIT]

    return pl.pallas_call(
        kernel,
        out_shape=jax.ShapeDtypeStruct((UNIT, *x.shape[1:]), x.dtype),
        in_specs=[VMEM],
        out_specs=VMEM,
        compiler_params=pltpu.CompilerParams(vmem_limit_bytes=VMEM_LIMIT),
        cost_estimate=cost(0, 2 * x.size),
    )(x)


def spread(x, along, unit, tokens=()):
    ahead, behind = along(x, 1), along(x, -1)
    if tokens and unit == 0:
        ahead = after(ahead, *tokens)
    elif tokens:
        behind = after(behind, *tokens)
    across = along(ahead, 1) if unit == 0 else along(behind, -1)
    return [(ahead, 1), (behind, 3), (across, 2)]


def exchange_z(x, step):
    return move(x, lambda z, core, y, u: (z ^ 1 if core == step else 3 - z, core, y, u))


def shards(gradient, momentum, params, bands):
    rep, fsdp = lax.axis_index("rep"), lax.axis_index("fsdp")
    place = jnp.stack(
        [lax.shift_right_logical(rep, 1), lax.shift_right_logical(fsdp, 2), fsdp & 3, rep & 1]
    ).astype(jnp.int32)
    table = cosine_table()
    forward = split_table(np.kron(np.eye(WIDE // GROUP), table.T))
    inverse = split_table(np.kron(np.eye(WIDE // GROUP), table))
    blocks = HALF // GROUP
    by_layer = jnp.transpose(bands[0], (0, 3, 1, 2)).reshape(LAYERS, 2, ROWS_HERE, 2, blocks)
    by_layer = jnp.pad(jnp.transpose(by_layer, (0, 1, 3, 2, 4)), ((0, 0),) * 4 + ((0, LANES - blocks),))

    gradient, momentum, params, forward, inverse = (
        pltpu.with_memory_space_constraint(x, pltpu.HBM) for x in (gradient, momentum, params, forward, inverse)
    )
    theirs, own_gradient, own_momentum, own_params, forward_here, inverse_here = pick_theirs(
        place, by_layer, gradient, momentum, params, forward, inverse
    )
    received = swap(theirs)
    mine = pick_own(place, by_layer, own_gradient, own_momentum, forward_here)
    chips = chip_sums(mine, received)
    two_chips = [pair_sum(chip, exchange_z(chip, 0)) for chip in chips]
    everyone = [exchange_z(block, 1) for block in two_chips]
    updated = []
    for unit in range(UNITS):
        updated.append(decode(two_chips[unit], everyone[unit], own_params, inverse_here, unit, two_chips[unit + 1 :]))

    first = []
    for unit, block in enumerate(updated):
        first.append([(block, 0)] + spread(block, along_first, unit, updated[unit + 1 :]))
    own = bring_together(place, first)

    new_momentum, tokens = None, []
    for unit in range(UNITS):
        new_momentum, token = keep_rest(
            place, by_layer, gradient, momentum, forward_here, inverse_here, unit, new_momentum, [own]
        )
        tokens.append(token)

    ahead, behind = along_second(own, 1), along_second(own, -1)
    ahead, behind = after(ahead, *tokens), after(behind, *tokens)
    across = [along_second(part(ahead, 0), 1), along_second(part(behind, 1), -1)]
    near = [(own, 0), (ahead, 1), (behind, 3)]
    others = [(swap(copied(own, behind)), 0), (swap(ahead), 1), (swap(behind), 3)]
    items = [(block, 0, steps, 0) for block, steps in near] + [(block, 0, steps, 1) for block, steps in others]
    whole, token = write_blocks(place, None, items)
    across = [after(block, token) for block in across]
    others = [swap(block) for block in across]
    for other, blocks in enumerate((across, others)):
        whole, _ = write_blocks(place, whole, [(block, unit * UNIT, 2, other) for unit, block in enumerate(blocks)])
    return new_momentum, whole.reshape(LAYERS, 16 * ROWS_HERE, WIDTH)


def solution(mesh):
    in_specs = (
        P("rep", None, "fsdp", None),
        P("rep", None, "fsdp", None),
        P(None, "fsdp", None),
        P("rep", None, "fsdp", None, None),
    )
    out_specs = (P("rep", None, "fsdp", None), P())
    return jax.shard_map(shards, mesh=mesh, in_specs=in_specs, out_specs=out_specs, check_vma=False)
```

```python
import math

import jax
import jax.numpy as jnp
import numpy as np
from jax import lax
from jax.experimental import pallas as pl
from jax.experimental.pallas import tpu as pltpu
from jax.sharding import PartitionSpec as P

GROUP = 64
BANDS = 8
LAYERS = 4
ROWS_HERE = 8
WIDTH = 13824
HALF = WIDTH // 2
WIDE = 256
LANES = 128
REPS = 8
BLOCKS = WIDTH // GROUP
UNIT = 2
UNITS = LAYERS // UNIT

decay_rate = 0.9
step_size = 1.0
VMEM_LIMIT = 16 * 1024 * 1024
VMEM_FIRST = 16 * 1024 * 1024


def cosine_table():
    k = np.arange(GROUP, dtype=np.float64)
    n = np.arange(GROUP, dtype=np.float64)
    scale = np.where(k == 0, math.sqrt(1.0 / GROUP), math.sqrt(2.0 / GROUP))
    return scale[:, None] * np.cos(math.pi * (2.0 * n[None, :] + 1.0) * k[:, None] / (2.0 * GROUP))


def split_table(table):
    high = jnp.asarray(table, jnp.float32).astype(jnp.bfloat16)
    low = (jnp.asarray(table, jnp.float32) - high.astype(jnp.float32)).astype(jnp.bfloat16)
    return jnp.stack([high, low])


def dot3(x, table_ref):
    high = x.astype(jnp.bfloat16)
    low = (x - high.astype(jnp.float32)).astype(jnp.bfloat16)
    total = jnp.dot(high, table_ref[1], preferred_element_type=jnp.float32)
    total += jnp.dot(low, table_ref[0], preferred_element_type=jnp.float32)
    return total + jnp.dot(high, table_ref[0], preferred_element_type=jnp.float32)


def stacked(x):
    return jnp.concatenate([x[:, at : at + WIDE] for at in range(0, x.shape[1], WIDE)], axis=0)


def pick_tiles(bands_ref, side, layers, spectra):
    lane = lax.broadcasted_iota(jnp.int32, (ROWS_HERE, LANES), 1)
    upper = lax.shift_right_logical(lane, 6)
    band = lax.bitwise_and(lax.shift_right_logical(lane, 3), 7)
    tiles = {}
    for i, layer in enumerate(layers):
        first_bands = bands_ref[layer, 0, side]
        second_bands = bands_ref[layer, 1, side]
        for tile in range(HALF // LANES):
            index = upper + (2 * tile + jnp.where(side == 0, 0, LANES - BLOCKS // 2))
            first = jnp.take_along_axis(first_bands, index, axis=1)
            second = jnp.take_along_axis(second_bands, index, axis=1)
            row = (i * (HALF // WIDE) + tile // 2) * ROWS_HERE
            column = (tile % 2) * LANES
            values = spectra[row : row + ROWS_HERE, column : column + LANES]
            tiles[i, tile] = jnp.where((first == band) | (second == band), values, 0.0)
    return tiles


def merged_rows(gradient, momentum):
    merged = decay_rate * momentum + gradient.astype(jnp.float32)
    return jnp.concatenate([stacked(merged[i]) for i in range(merged.shape[0])], axis=0)


HBM = pl.BlockSpec(memory_space=pl.ANY)
VMEM = pl.BlockSpec(memory_space=pltpu.VMEM)
SMEM = pl.BlockSpec(memory_space=pltpu.SMEM)
HALF_UNIT = jax.ShapeDtypeStruct((UNIT, ROWS_HERE, HALF), jnp.bfloat16)
HALF_LAYERS = jax.ShapeDtypeStruct((LAYERS, ROWS_HERE, HALF), jnp.bfloat16)
HALF_MOMENTUM = jax.ShapeDtypeStruct((LAYERS, ROWS_HERE, HALF), jnp.float32)
TABLE = jax.ShapeDtypeStruct((2, WIDE, WIDE), jnp.bfloat16)
SIDE_BANDS = jax.ShapeDtypeStruct((LAYERS, 2, 2, ROWS_HERE, LANES), jnp.int32)
TOKEN = jax.ShapeDtypeStruct((8, 128), jnp.float32)


def cost(flops, size):
    return pl.CostEstimate(flops=flops, bytes_accessed=size, transcendentals=0)


def store_picked(bands_ref, side, unit, spectra, out_ref):
    layers = range(unit * UNIT, unit * UNIT + UNIT)
    for (layer, tile), values in pick_tiles(bands_ref, side, layers, spectra).items():
        out_ref[unit * UNIT + layer, :, tile * LANES : (tile + 1) * LANES] = values.astype(jnp.bfloat16)


def pick_theirs(place, by_layer, gradient, momentum, params, forward, inverse):
    out_shapes = [HALF_LAYERS, HALF_LAYERS, HALF_MOMENTUM, HALF_LAYERS, TABLE, TABLE, SIDE_BANDS]

    def kernel(place_ref, raw_ref, gradient_ref, momentum_ref, params_ref, forward_ref, inverse_ref, *refs):
        picked, own_gradient, own_momentum, own_params, table, back_table, bands_ref = refs[:7]
        gradients, momenta, raw, sems = refs[7:]
        core = place_ref[3]
        own = pl.ds(pl.multiple_of(core * HALF, LANES), HALF)
        theirs = pl.ds(pl.multiple_of((1 - core) * HALF, LANES), HALF)
        pairs = [(forward_ref, table)]
        for unit in range(UNITS):
            layers = pl.ds(unit * UNIT, UNIT)
            pairs.append((gradient_ref.at[0, layers, :, theirs], gradients.at[layers]))
            pairs.append((momentum_ref.at[0, layers, :, theirs], momenta.at[layers]))
        pairs.append((gradient_ref.at[0, :, :, own], own_gradient))
        pairs.append((momentum_ref.at[0, :, :, own], own_momentum))
        pairs.append((params_ref.at[:, :, own], own_params))
        pairs.append((inverse_ref, back_table))
        pairs.insert(0, (raw_ref, raw))
        copies = [pltpu.make_async_copy(src, dst, sems.at[i]) for i, (src, dst) in enumerate(pairs)]
        for copy in copies:
            copy.start()
        copies[0].wait()
        for layer in range(LAYERS):
            both = raw[layer]
            for i in range(2):
                bands_ref[layer, i, 0] = both[:, i, :LANES]
                bands_ref[layer, i, 1] = both[:, i, BLOCKS - LANES :]
        copies.pop(0)
        copies[0].wait()
        for unit in range(UNITS):
            copies[1 + 2 * unit].wait()
            copies[2 + 2 * unit].wait()
            layers = slice(unit * UNIT, unit * UNIT + UNIT)
            spectra = dot3(merged_rows(gradients[layers], momenta[layers]), table)
            store_picked(bands_ref, 1 - core, unit, spectra, picked)
        for copy in copies[1 + 2 * UNITS :]:
            copy.wait()

    return pl.pallas_call(
        kernel,
        out_shape=out_shapes,
        in_specs=[SMEM] + [HBM] * 6,
        out_specs=[VMEM] * len(out_shapes),
        scratch_shapes=[
            pltpu.VMEM((LAYERS, ROWS_HERE, HALF), jnp.bfloat16),
            pltpu.VMEM((LAYERS, ROWS_HERE, HALF), jnp.float32),
            pltpu.VMEM((LAYERS, ROWS_HERE, 2, BLOCKS), jnp.int32),
            pltpu.SemaphoreType.DMA((6 + 2 * UNITS,)),
        ],
        compiler_params=pltpu.CompilerParams(vmem_limit_bytes=VMEM_FIRST),
        cost_estimate=cost(6 * LAYERS * ROWS_HERE * HALF * WIDE, 6000000),
    )(place, by_layer, gradient, momentum, params, forward, inverse)


def pick_own(place, by_layer, gradient, momentum, forward):
    def kernel(place_ref, bands_ref, gradient_ref, momentum_ref, table_ref, picked):
        for unit in range(UNITS):
            layers = slice(unit * UNIT, unit * UNIT + UNIT)
            spectra = dot3(merged_rows(gradient_ref[layers], momentum_ref[layers]), table_ref)
            store_picked(bands_ref, place_ref[3], unit, spectra, picked)

    return pl.pallas_call(
        kernel,
        out_shape=HALF_LAYERS,
        in_specs=[SMEM] + [VMEM] * 4,
        out_specs=VMEM,
        compiler_params=pltpu.CompilerParams(vmem_limit_bytes=VMEM_LIMIT),
        cost_estimate=cost(6 * LAYERS * ROWS_HERE * HALF * WIDE, 2000000),
    )(place, by_layer, gradient, momentum, forward)


def chip_sums(mine, received):
    def kernel(mine_ref, received_ref, *outs):
        for unit, out_ref in enumerate(outs):
            layers = slice(unit * UNIT, (unit + 1) * UNIT)
            total = mine_ref[layers].astype(jnp.float32) + received_ref[layers].astype(jnp.float32)
            out_ref[...] = total.astype(jnp.bfloat16)

    return pl.pallas_call(
        kernel,
        out_shape=[HALF_UNIT] * UNITS,
        in_specs=[VMEM] * 2,
        out_specs=[VMEM] * UNITS,
        compiler_params=pltpu.CompilerParams(vmem_limit_bytes=VMEM_LIMIT),
        cost_estimate=cost(0, 1400000),
    )(mine, received)


def pair_sum(mine, received, tokens=()):
    def kernel(mine_ref, received_ref, *refs):
        total = mine_ref[...].astype(jnp.float32) + received_ref[...].astype(jnp.float32)
        refs[-1][...] = total.astype(jnp.bfloat16)

    return pl.pallas_call(
        kernel,
        out_shape=HALF_UNIT,
        in_specs=[VMEM] * (2 + len(tokens)),
        out_specs=VMEM,
        compiler_params=pltpu.CompilerParams(vmem_limit_bytes=VMEM_LIMIT),
        cost_estimate=cost(0, 700000),
    )(mine, received, *tokens)


def keep_rest(place, by_layer, gradient, momentum, forward, inverse, unit, before, tokens=()):
    def kernel(bands_ref, gradient_ref, momentum_ref, forward_ref, inverse_ref, *refs):
        out_ref, token_ref, gradients, momenta, table, sems = refs[-6:]
        token_ref[...] = jnp.zeros_like(token_ref)
        layers = pl.ds(unit * UNIT, UNIT)
        pairs = [(forward_ref, table)]
        for side in range(2):
            columns = pl.ds(side * HALF, HALF)
            pairs.append((gradient_ref.at[0, layers, :, columns], gradients.at[side]))
            pairs.append((momentum_ref.at[0, layers, :, columns], momenta.at[side]))
        copies = [pltpu.make_async_copy(src, dst, sems.at[i]) for i, (src, dst) in enumerate(pairs)]
        for copy in copies:
            copy.start()
        copies[0].wait()
        for side in range(2):
            copies[1 + 2 * side].wait()
            copies[2 + 2 * side].wait()
            merged = merged_rows(gradients[side], momenta[side])
            spectra = dot3(merged, table)
            tiles = pick_tiles(bands_ref, side, range(unit * UNIT, unit * UNIT + UNIT), spectra)
            wide = [
                jnp.concatenate([tiles[i, at], tiles[i, at + 1]], axis=1)
                for i in range(UNIT)
                for at in range(0, HALF // LANES, 2)
            ]
            kept = merged - dot3(jnp.concatenate(wide, axis=0), inverse_ref)
            for i in range(UNIT):
                for at in range(HALF // WIDE):
                    row = (i * (HALF // WIDE) + at) * ROWS_HERE
                    momenta[side, i, :, at * WIDE : (at + 1) * WIDE] = kept[row : row + ROWS_HERE]
            target = out_ref.at[0, layers, :, pl.ds(side * HALF, HALF)]
            copies.append(pltpu.make_async_copy(momenta.at[side], target, sems.at[5 + side]))
            copies[-1].start()
        copies[-2].wait()
        copies[-1].wait()

    operands = [by_layer, gradient, momentum, forward, inverse, *tokens]
    specs = [VMEM, HBM, HBM, HBM, VMEM] + [VMEM] * len(tokens)
    aliases = {}
    if before is not None:
        aliases = {len(operands): 0}
        operands.append(before)
        specs.append(HBM)
    return pl.pallas_call(
        kernel,
        out_shape=[jax.ShapeDtypeStruct(momentum.shape, jnp.float32), TOKEN],
        in_specs=specs,
        out_specs=[HBM, VMEM],
        scratch_shapes=[
            pltpu.VMEM((2, UNIT, ROWS_HERE, HALF), jnp.bfloat16),
            pltpu.VMEM((2, UNIT, ROWS_HERE, HALF), jnp.float32),
            pltpu.VMEM((2, WIDE, WIDE), jnp.bfloat16),
            pltpu.SemaphoreType.DMA((7,)),
        ],
        input_output_aliases=aliases,
        compiler_params=pltpu.CompilerParams(vmem_limit_bytes=VMEM_LIMIT),
        cost_estimate=cost(12 * UNIT * ROWS_HERE * WIDTH * WIDE, 3000000),
    )(*operands)


def decode(mine, received, params, inverse, unit, tokens=()):
    def kernel(mine_ref, received_ref, params_ref, inverse_ref, *refs):
        total = mine_ref[...].astype(jnp.float32) + received_ref[...].astype(jnp.float32)
        total = total * (1.0 / REPS)
        restored = jnp.concatenate([stacked(total[i]) for i in range(UNIT)], axis=0)
        decoded = dot3(restored, inverse_ref)
        for i in range(UNIT):
            for at in range(HALF // WIDE):
                columns = slice(at * WIDE, (at + 1) * WIDE)
                row = (i * (HALF // WIDE) + at) * ROWS_HERE
                change = step_size * decoded[row : row + ROWS_HERE]
                updated = params_ref[unit * UNIT + i, :, columns].astype(jnp.float32) - change
                refs[-1][i, :, columns] = updated.astype(jnp.bfloat16)

    return pl.pallas_call(
        kernel,
        out_shape=HALF_UNIT,
        in_specs=[VMEM] * (4 + len(tokens)),
        out_specs=VMEM,
        compiler_params=pltpu.CompilerParams(vmem_limit_bytes=VMEM_LIMIT),
        cost_estimate=cost(6 * UNIT * ROWS_HERE * HALF * WIDE, 1500000),
    )(mine, received, params, inverse, *tokens)


def first_place(place_ref):
    return jnp.where(place_ref[3] == 0, place_ref[2], place_ref[1])


def second_place(place_ref):
    return jnp.where(place_ref[3] == 0, place_ref[1], place_ref[2])


def bring_together(place, units):
    blocks = [block for unit in units for block, _ in unit]

    def kernel(place_ref, *refs):
        here = first_place(place_ref)
        ins = iter(refs)
        for at, unit in enumerate(units):
            for _, steps in unit:
                refs[-1][at * UNIT : (at + 1) * UNIT, lax.rem(here + (4 - steps), 4)] = next(ins)[...]

    return pl.pallas_call(
        kernel,
        out_shape=jax.ShapeDtypeStruct((LAYERS, 4, ROWS_HERE, HALF), jnp.bfloat16),
        in_specs=[SMEM] + [VMEM] * len(blocks),
        out_specs=VMEM,
        compiler_params=pltpu.CompilerParams(vmem_limit_bytes=VMEM_LIMIT),
        cost_estimate=cost(0, 3600000),
    )(place, *blocks)


def write_blocks(place, whole, items):
    blocks = [item[0] for item in items]

    def kernel(place_ref, *refs):
        ins, (out, token_ref, sems) = refs[: len(blocks)], refs[-3:]
        token_ref[...] = jnp.zeros_like(token_ref)
        y, x, core = place_ref[1], place_ref[2], place_ref[3]
        copies = []
        for block, (_, first_layer, steps, other) in zip(ins, items):
            side = core if other == 0 else 1 - core
            columns = pl.ds(pl.multiple_of(side * HALF, LANES), HALF)
            here = lax.rem(jnp.where(side == 0, y, x) + (4 - steps), 4)
            for i in range(4):
                rows = jnp.where(side == 0, 4 * here + i, 4 * i + here)
                for layer in range(block.shape[0]):
                    target = out.at[first_layer + layer, rows, :, columns]
                    copies.append(pltpu.make_async_copy(block.at[layer, i], target, sems.at[len(copies)]))
        for copy in copies:
            copy.start()
        for copy in copies:
            copy.wait()

    operands = [place] + blocks
    specs = [SMEM] + [VMEM] * len(blocks)
    aliases = {}
    if whole is not None:
        aliases = {len(operands): 0}
        operands.append(whole)
        specs.append(HBM)
    return pl.pallas_call(
        kernel,
        out_shape=[jax.ShapeDtypeStruct((LAYERS, 16, ROWS_HERE, WIDTH), jnp.bfloat16), TOKEN],
        in_specs=specs,
        out_specs=[HBM, VMEM],
        scratch_shapes=[pltpu.SemaphoreType.DMA((4 * sum(block.shape[0] for block in blocks),))],
        input_output_aliases=aliases,
        compiler_params=pltpu.CompilerParams(vmem_limit_bytes=VMEM_LIMIT),
        cost_estimate=cost(0, 2 * sum(b.size * 2 for b in blocks)),
    )(*operands)


def move(x, step):
    pairs = []
    for device in range(128):
        z, core, y, u = device // 32, device // 16 % 2, device // 4 % 4, device % 4
        z, core, y, u = step(z, core, y, u)
        pairs.append((device, (z % 4 * 2 + core) * 16 + y % 4 * 4 + u % 4))
    return lax.ppermute(x, ("rep", "fsdp"), pairs)


def swap(x):
    return move(x, lambda z, core, y, u: (z, 1 - core, y, u))


def along_first(x, by):
    return move(x, lambda z, core, y, u: (z, core, y, u + by) if core == 0 else (z, core, y + by, u))


def along_second(x, by):
    return move(x, lambda z, core, y, u: (z, core, y + by, u) if core == 0 else (z, core, y, u + by))


def after(x, *tokens):
    def kernel(x_ref, *refs):
        pass

    return pl.pallas_call(
        kernel,
        out_shape=jax.ShapeDtypeStruct(x.shape, x.dtype),
        in_specs=[VMEM] * (1 + len(tokens)),
        out_specs=VMEM,
        input_output_aliases={0: 0},
        compiler_params=pltpu.CompilerParams(vmem_limit_bytes=VMEM_LIMIT),
        cost_estimate=cost(0, 4096),
    )(x, *tokens)


def copied(x, token):
    def kernel(x_ref, token_ref, out_ref):
        out_ref[...] = x_ref[...]

    return pl.pallas_call(
        kernel,
        out_shape=jax.ShapeDtypeStruct(x.shape, x.dtype),
        in_specs=[VMEM] * 2,
        out_specs=VMEM,
        compiler_params=pltpu.CompilerParams(vmem_limit_bytes=VMEM_LIMIT),
        cost_estimate=cost(0, 2 * x.size * 2),
    )(x, token)


def part(x, unit):
    def kernel(x_ref, *refs):
        refs[-1][...] = x_ref[unit * UNIT : (unit + 1) * UNIT]

    return pl.pallas_call(
        kernel,
        out_shape=jax.ShapeDtypeStruct((UNIT, *x.shape[1:]), x.dtype),
        in_specs=[VMEM],
        out_specs=VMEM,
        compiler_params=pltpu.CompilerParams(vmem_limit_bytes=VMEM_LIMIT),
        cost_estimate=cost(0, 2 * x.size),
    )(x)


def spread(x, along):
    return [(along(x, 1), 1), (along(x, -1), 3), (along(x, 2), 2)]


def exchange_z(x, step):
    return move(x, lambda z, core, y, u: (z ^ 1 if core == step else 3 - z, core, y, u))


def shards(gradient, momentum, params, bands):
    rep, fsdp = lax.axis_index("rep"), lax.axis_index("fsdp")
    place = jnp.stack(
        [lax.shift_right_logical(rep, 1), lax.shift_right_logical(fsdp, 2), fsdp & 3, rep & 1]
    ).astype(jnp.int32)
    table = cosine_table()
    forward = split_table(np.kron(np.eye(WIDE // GROUP), table.T))
    inverse = split_table(np.kron(np.eye(WIDE // GROUP), table))
    by_layer = jnp.transpose(bands[0], (0, 1, 3, 2))
    gradient, momentum, params, forward, inverse, by_layer = (
        pltpu.with_memory_space_constraint(x, pltpu.HBM)
        for x in (gradient, momentum, params, forward, inverse, by_layer)
    )
    theirs, own_gradient, own_momentum, own_params, forward_here, inverse_here, by_layer = pick_theirs(
        place, by_layer, gradient, momentum, params, forward, inverse
    )
    received = swap(theirs)
    mine = pick_own(place, by_layer, own_gradient, own_momentum, forward_here)
    chips = chip_sums(mine, received)
    two_chips = [pair_sum(chip, exchange_z(chip, 0)) for chip in chips]
    everyone = [exchange_z(block, 1) for block in two_chips]
    updated = []
    for unit in range(UNITS):
        updated.append(decode(two_chips[unit], everyone[unit], own_params, inverse_here, unit, two_chips[unit + 1 :]))

    first = []
    for unit, block in enumerate(updated):
        first.append([(block, 0)] + spread(block, along_first))
    own = bring_together(place, first)

    new_momentum, tokens = None, []
    for unit in range(UNITS):
        new_momentum, token = keep_rest(
            place, by_layer, gradient, momentum, forward_here, inverse_here, unit, new_momentum, [own]
        )
        tokens.append(token)

    ahead, behind = along_second(own, 1), along_second(own, -1)
    whole, token = write_blocks(place, None, [(own, 0, 0, 0)])
    tokens.append(token)
    ahead, behind = after(ahead, *tokens), after(behind, *tokens)
    across = [along_second(part(ahead, 0), 1), along_second(part(behind, 1), -1)]
    items = [(ahead, 0, 1, 0), (behind, 0, 3, 0), (swap(ahead), 0, 1, 1), (swap(behind), 0, 3, 1)]
    whole, token = write_blocks(place, whole, items)
    items = [(swap(copied(own, token)), 0, 0, 1)]
    for unit, block in enumerate(across):
        block = after(block, token)
        items += [(block, unit * UNIT, 2, 0), (swap(block), unit * UNIT, 2, 1)]
    whole, _ = write_blocks(place, whole, items)
    return new_momentum, whole.reshape(LAYERS, 16 * ROWS_HERE, WIDTH)


def solution(mesh):
    in_specs = (
        P("rep", None, "fsdp", None),
        P("rep", None, "fsdp", None),
        P(None, "fsdp", None),
        P("rep", None, "fsdp", None, None),
    )
    out_specs = (P("rep", None, "fsdp", None), P())
    return jax.shard_map(shards, mesh=mesh, in_specs=in_specs, out_specs=out_specs, check_vma=False)
```

```python
import math

import jax
import jax.numpy as jnp
import numpy as np
from jax import lax
from jax.experimental import pallas as pl
from jax.experimental.pallas import tpu as pltpu
from jax.sharding import PartitionSpec as P

GROUP = 64
BANDS = 8
LAYERS = 4
ROWS_HERE = 8
WIDTH = 13824
HALF = WIDTH // 2
WIDE = 256
LANES = 128
REPS = 8
BLOCKS = WIDTH // GROUP
UNIT = 2
UNITS = LAYERS // UNIT

decay_rate = 0.9
step_size = 1.0
VMEM_LIMIT = 16 * 1024 * 1024
VMEM_FIRST = 16 * 1024 * 1024


def cosine_table():
    k = np.arange(GROUP, dtype=np.float64)
    n = np.arange(GROUP, dtype=np.float64)
    scale = np.where(k == 0, math.sqrt(1.0 / GROUP), math.sqrt(2.0 / GROUP))
    return scale[:, None] * np.cos(math.pi * (2.0 * n[None, :] + 1.0) * k[:, None] / (2.0 * GROUP))


def split_table(table):
    high = jnp.asarray(table, jnp.float32).astype(jnp.bfloat16)
    low = (jnp.asarray(table, jnp.float32) - high.astype(jnp.float32)).astype(jnp.bfloat16)
    return jnp.stack([high, low])


def dot3(x, table_ref):
    high = x.astype(jnp.bfloat16)
    low = (x - high.astype(jnp.float32)).astype(jnp.bfloat16)
    total = jnp.dot(high, table_ref[1], preferred_element_type=jnp.float32)
    total += jnp.dot(low, table_ref[0], preferred_element_type=jnp.float32)
    return total + jnp.dot(high, table_ref[0], preferred_element_type=jnp.float32)


def stacked(x):
    return jnp.concatenate([x[:, at : at + WIDE] for at in range(0, x.shape[1], WIDE)], axis=0)


def pick_tiles(bands_ref, side, layers, spectra):
    lane = lax.broadcasted_iota(jnp.int32, (ROWS_HERE, LANES), 1)
    upper = lax.shift_right_logical(lane, 6)
    bit = lax.shift_left(jnp.ones_like(lane), lax.bitwise_and(lax.shift_right_logical(lane, 3), 7))
    tiles = {}
    for i, layer in enumerate(layers):
        chosen = bands_ref[layer, side]
        for tile in range(HALF // LANES):
            index = upper + (2 * tile + jnp.where(side == 0, 0, LANES - BLOCKS // 2))
            here = jnp.take_along_axis(chosen, index, axis=1)
            row = (i * (HALF // WIDE) + tile // 2) * ROWS_HERE
            column = (tile % 2) * LANES
            values = spectra[row : row + ROWS_HERE, column : column + LANES]
            tiles[i, tile] = jnp.where(lax.bitwise_and(here, bit) != 0, values, 0.0)
    return tiles


def merged_rows(gradient, momentum):
    merged = decay_rate * momentum + gradient.astype(jnp.float32)
    return jnp.concatenate([stacked(merged[i]) for i in range(merged.shape[0])], axis=0)


HBM = pl.BlockSpec(memory_space=pl.ANY)
VMEM = pl.BlockSpec(memory_space=pltpu.VMEM)
SMEM = pl.BlockSpec(memory_space=pltpu.SMEM)
HALF_UNIT = jax.ShapeDtypeStruct((UNIT, ROWS_HERE, HALF), jnp.bfloat16)
HALF_LAYERS = jax.ShapeDtypeStruct((LAYERS, ROWS_HERE, HALF), jnp.bfloat16)
HALF_MOMENTUM = jax.ShapeDtypeStruct((LAYERS, ROWS_HERE, HALF), jnp.float32)
TABLE = jax.ShapeDtypeStruct((2, WIDE, WIDE), jnp.bfloat16)
SIDE_BANDS = jax.ShapeDtypeStruct((LAYERS, 2, ROWS_HERE, LANES), jnp.int32)
TOKEN = jax.ShapeDtypeStruct((8, 128), jnp.float32)


def cost(flops, size):
    return pl.CostEstimate(flops=flops, bytes_accessed=size, transcendentals=0)


def store_picked(bands_ref, side, unit, spectra, out_ref):
    layers = range(unit * UNIT, unit * UNIT + UNIT)
    for (layer, tile), values in pick_tiles(bands_ref, side, layers, spectra).items():
        out_ref[unit * UNIT + layer, :, tile * LANES : (tile + 1) * LANES] = values.astype(jnp.bfloat16)


def pick_theirs(place, by_layer, gradient, momentum, params, forward, inverse):
    out_shapes = [HALF_LAYERS, HALF_LAYERS, HALF_MOMENTUM, HALF_LAYERS, TABLE, TABLE, SIDE_BANDS]

    def kernel(place_ref, raw_ref, gradient_ref, momentum_ref, params_ref, forward_ref, inverse_ref, *refs):
        picked, own_gradient, own_momentum, own_params, table, back_table, bands_ref = refs[:7]
        gradients, momenta, raw, sems = refs[7:]
        core = place_ref[3]
        own = pl.ds(pl.multiple_of(core * HALF, LANES), HALF)
        theirs = pl.ds(pl.multiple_of((1 - core) * HALF, LANES), HALF)
        pairs = [(forward_ref, table)]
        for unit in range(UNITS):
            layers = pl.ds(unit * UNIT, UNIT)
            pairs.append((gradient_ref.at[0, layers, :, theirs], gradients.at[layers]))
            pairs.append((momentum_ref.at[0, layers, :, theirs], momenta.at[layers]))
        pairs.append((gradient_ref.at[0, :, :, own], own_gradient))
        pairs.append((momentum_ref.at[0, :, :, own], own_momentum))
        pairs.append((params_ref.at[:, :, own], own_params))
        pairs.append((inverse_ref, back_table))
        pairs.insert(0, (raw_ref, raw))
        copies = [pltpu.make_async_copy(src, dst, sems.at[i]) for i, (src, dst) in enumerate(pairs)]
        for copy in copies:
            copy.start()
        copies[0].wait()
        for layer in range(LAYERS):
            both = raw[layer]
            bits = lax.shift_left(jnp.ones_like(both), both)
            bits = lax.bitwise_or(bits[:, 0], bits[:, 1])
            bands_ref[layer, 0] = bits[:, :LANES]
            bands_ref[layer, 1] = bits[:, BLOCKS - LANES :]
        copies.pop(0)
        copies[0].wait()
        for unit in range(UNITS):
            copies[1 + 2 * unit].wait()
            copies[2 + 2 * unit].wait()
            layers = slice(unit * UNIT, unit * UNIT + UNIT)
            spectra = dot3(merged_rows(gradients[layers], momenta[layers]), table)
            store_picked(bands_ref, 1 - core, unit, spectra, picked)
        for copy in copies[1 + 2 * UNITS :]:
            copy.wait()

    return pl.pallas_call(
        kernel,
        out_shape=out_shapes,
        in_specs=[SMEM] + [HBM] * 6,
        out_specs=[VMEM] * len(out_shapes),
        scratch_shapes=[
            pltpu.VMEM((LAYERS, ROWS_HERE, HALF), jnp.bfloat16),
            pltpu.VMEM((LAYERS, ROWS_HERE, HALF), jnp.float32),
            pltpu.VMEM((LAYERS, ROWS_HERE, 2, BLOCKS), jnp.int32),
            pltpu.SemaphoreType.DMA((6 + 2 * UNITS,)),
        ],
        compiler_params=pltpu.CompilerParams(vmem_limit_bytes=VMEM_FIRST),
        cost_estimate=cost(6 * LAYERS * ROWS_HERE * HALF * WIDE, 6000000),
    )(place, by_layer, gradient, momentum, params, forward, inverse)


def pick_own(place, by_layer, gradient, momentum, forward):
    def kernel(place_ref, bands_ref, gradient_ref, momentum_ref, table_ref, picked):
        for unit in range(UNITS):
            layers = slice(unit * UNIT, unit * UNIT + UNIT)
            spectra = dot3(merged_rows(gradient_ref[layers], momentum_ref[layers]), table_ref)
            store_picked(bands_ref, place_ref[3], unit, spectra, picked)

    return pl.pallas_call(
        kernel,
        out_shape=HALF_LAYERS,
        in_specs=[SMEM] + [VMEM] * 4,
        out_specs=VMEM,
        compiler_params=pltpu.CompilerParams(vmem_limit_bytes=VMEM_LIMIT),
        cost_estimate=cost(6 * LAYERS * ROWS_HERE * HALF * WIDE, 2000000),
    )(place, by_layer, gradient, momentum, forward)


def chip_sums(mine, received):
    def kernel(mine_ref, received_ref, *outs):
        for unit, out_ref in enumerate(outs):
            layers = slice(unit * UNIT, (unit + 1) * UNIT)
            total = mine_ref[layers].astype(jnp.float32) + received_ref[layers].astype(jnp.float32)
            out_ref[...] = total.astype(jnp.bfloat16)

    return pl.pallas_call(
        kernel,
        out_shape=[HALF_UNIT] * UNITS,
        in_specs=[VMEM] * 2,
        out_specs=[VMEM] * UNITS,
        compiler_params=pltpu.CompilerParams(vmem_limit_bytes=VMEM_LIMIT),
        cost_estimate=cost(0, 1400000),
    )(mine, received)


def pair_sum(mine, received, tokens=()):
    def kernel(mine_ref, received_ref, *refs):
        total = mine_ref[...].astype(jnp.float32) + received_ref[...].astype(jnp.float32)
        refs[-1][...] = total.astype(jnp.bfloat16)

    return pl.pallas_call(
        kernel,
        out_shape=HALF_UNIT,
        in_specs=[VMEM] * (2 + len(tokens)),
        out_specs=VMEM,
        compiler_params=pltpu.CompilerParams(vmem_limit_bytes=VMEM_LIMIT),
        cost_estimate=cost(0, 700000),
    )(mine, received, *tokens)


def keep_rest(place, by_layer, gradient, momentum, forward, inverse, unit, before, tokens=()):
    def kernel(bands_ref, gradient_ref, momentum_ref, forward_ref, inverse_ref, *refs):
        out_ref, token_ref, gradients, momenta, table, sems = refs[-6:]
        token_ref[...] = jnp.zeros_like(token_ref)
        layers = pl.ds(unit * UNIT, UNIT)
        pairs = [(forward_ref, table)]
        for side in range(2):
            columns = pl.ds(side * HALF, HALF)
            pairs.append((gradient_ref.at[0, layers, :, columns], gradients.at[side]))
            pairs.append((momentum_ref.at[0, layers, :, columns], momenta.at[side]))
        copies = [pltpu.make_async_copy(src, dst, sems.at[i]) for i, (src, dst) in enumerate(pairs)]
        for copy in copies:
            copy.start()
        copies[0].wait()
        for side in range(2):
            copies[1 + 2 * side].wait()
            copies[2 + 2 * side].wait()
            merged = merged_rows(gradients[side], momenta[side])
            spectra = dot3(merged, table)
            tiles = pick_tiles(bands_ref, side, range(unit * UNIT, unit * UNIT + UNIT), spectra)
            wide = [
                jnp.concatenate([tiles[i, at], tiles[i, at + 1]], axis=1)
                for i in range(UNIT)
                for at in range(0, HALF // LANES, 2)
            ]
            kept = merged - dot3(jnp.concatenate(wide, axis=0), inverse_ref)
            for i in range(UNIT):
                for at in range(HALF // WIDE):
                    row = (i * (HALF // WIDE) + at) * ROWS_HERE
                    momenta[side, i, :, at * WIDE : (at + 1) * WIDE] = kept[row : row + ROWS_HERE]
            target = out_ref.at[0, layers, :, pl.ds(side * HALF, HALF)]
            copies.append(pltpu.make_async_copy(momenta.at[side], target, sems.at[5 + side]))
            copies[-1].start()
        copies[-2].wait()
        copies[-1].wait()

    operands = [by_layer, gradient, momentum, forward, inverse, *tokens]
    specs = [VMEM, HBM, HBM, HBM, VMEM] + [VMEM] * len(tokens)
    aliases = {}
    if before is not None:
        aliases = {len(operands): 0}
        operands.append(before)
        specs.append(HBM)
    return pl.pallas_call(
        kernel,
        out_shape=[jax.ShapeDtypeStruct(momentum.shape, jnp.float32), TOKEN],
        in_specs=specs,
        out_specs=[HBM, VMEM],
        scratch_shapes=[
            pltpu.VMEM((2, UNIT, ROWS_HERE, HALF), jnp.bfloat16),
            pltpu.VMEM((2, UNIT, ROWS_HERE, HALF), jnp.float32),
            pltpu.VMEM((2, WIDE, WIDE), jnp.bfloat16),
            pltpu.SemaphoreType.DMA((7,)),
        ],
        input_output_aliases=aliases,
        compiler_params=pltpu.CompilerParams(vmem_limit_bytes=VMEM_LIMIT),
        cost_estimate=cost(12 * UNIT * ROWS_HERE * WIDTH * WIDE, 3000000),
    )(*operands)


def decode(mine, received, params, inverse, unit, tokens=()):
    def kernel(mine_ref, received_ref, params_ref, inverse_ref, *refs):
        total = mine_ref[...].astype(jnp.float32) + received_ref[...].astype(jnp.float32)
        total = total * (1.0 / REPS)
        restored = jnp.concatenate([stacked(total[i]) for i in range(UNIT)], axis=0)
        decoded = dot3(restored, inverse_ref)
        for i in range(UNIT):
            for at in range(HALF // WIDE):
                columns = slice(at * WIDE, (at + 1) * WIDE)
                row = (i * (HALF // WIDE) + at) * ROWS_HERE
                change = step_size * decoded[row : row + ROWS_HERE]
                updated = params_ref[unit * UNIT + i, :, columns].astype(jnp.float32) - change
                refs[-1][i, :, columns] = updated.astype(jnp.bfloat16)

    return pl.pallas_call(
        kernel,
        out_shape=HALF_UNIT,
        in_specs=[VMEM] * (4 + len(tokens)),
        out_specs=VMEM,
        compiler_params=pltpu.CompilerParams(vmem_limit_bytes=VMEM_LIMIT),
        cost_estimate=cost(6 * UNIT * ROWS_HERE * HALF * WIDE, 1500000),
    )(mine, received, params, inverse, *tokens)


def first_place(place_ref):
    return jnp.where(place_ref[3] == 0, place_ref[2], place_ref[1])


def second_place(place_ref):
    return jnp.where(place_ref[3] == 0, place_ref[1], place_ref[2])


def bring_together(place, units):
    blocks = [block for unit in units for block, _ in unit]

    def kernel(place_ref, *refs):
        here = first_place(place_ref)
        ins = iter(refs)
        for at, unit in enumerate(units):
            for _, steps in unit:
                refs[-1][at * UNIT : (at + 1) * UNIT, lax.rem(here + (4 - steps), 4)] = next(ins)[...]

    return pl.pallas_call(
        kernel,
        out_shape=jax.ShapeDtypeStruct((LAYERS, 4, ROWS_HERE, HALF), jnp.bfloat16),
        in_specs=[SMEM] + [VMEM] * len(blocks),
        out_specs=VMEM,
        compiler_params=pltpu.CompilerParams(vmem_limit_bytes=VMEM_LIMIT),
        cost_estimate=cost(0, 3600000),
    )(place, *blocks)


def write_blocks(place, whole, items):
    blocks = [item[0] for item in items]

    def kernel(place_ref, *refs):
        ins, (out, token_ref, sems) = refs[: len(blocks)], refs[-3:]
        token_ref[...] = jnp.zeros_like(token_ref)
        y, x, core = place_ref[1], place_ref[2], place_ref[3]
        copies = []
        for block, (_, first_layer, steps, other) in zip(ins, items):
            side = core if other == 0 else 1 - core
            columns = pl.ds(pl.multiple_of(side * HALF, LANES), HALF)
            here = lax.rem(jnp.where(side == 0, y, x) + (4 - steps), 4)
            for i in range(4):
                rows = jnp.where(side == 0, 4 * here + i, 4 * i + here)
                for layer in range(block.shape[0]):
                    target = out.at[first_layer + layer, rows, :, columns]
                    copies.append(pltpu.make_async_copy(block.at[layer, i], target, sems.at[len(copies)]))
        for copy in copies:
            copy.start()
        for copy in copies:
            copy.wait()

    operands = [place] + blocks
    specs = [SMEM] + [VMEM] * len(blocks)
    aliases = {}
    if whole is not None:
        aliases = {len(operands): 0}
        operands.append(whole)
        specs.append(HBM)
    return pl.pallas_call(
        kernel,
        out_shape=[jax.ShapeDtypeStruct((LAYERS, 16, ROWS_HERE, WIDTH), jnp.bfloat16), TOKEN],
        in_specs=specs,
        out_specs=[HBM, VMEM],
        scratch_shapes=[pltpu.SemaphoreType.DMA((4 * sum(block.shape[0] for block in blocks),))],
        input_output_aliases=aliases,
        compiler_params=pltpu.CompilerParams(vmem_limit_bytes=VMEM_LIMIT),
        cost_estimate=cost(0, 2 * sum(b.size * 2 for b in blocks)),
    )(*operands)


def move(x, step):
    pairs = []
    for device in range(128):
        z, core, y, u = device // 32, device // 16 % 2, device // 4 % 4, device % 4
        z, core, y, u = step(z, core, y, u)
        pairs.append((device, (z % 4 * 2 + core) * 16 + y % 4 * 4 + u % 4))
    return lax.ppermute(x, ("rep", "fsdp"), pairs)


def swap(x):
    return move(x, lambda z, core, y, u: (z, 1 - core, y, u))


def along_first(x, by):
    return move(x, lambda z, core, y, u: (z, core, y, u + by) if core == 0 else (z, core, y + by, u))


def along_second(x, by):
    return move(x, lambda z, core, y, u: (z, core, y + by, u) if core == 0 else (z, core, y, u + by))


def after(x, *tokens):
    def kernel(x_ref, *refs):
        pass

    return pl.pallas_call(
        kernel,
        out_shape=jax.ShapeDtypeStruct(x.shape, x.dtype),
        in_specs=[VMEM] * (1 + len(tokens)),
        out_specs=VMEM,
        input_output_aliases={0: 0},
        compiler_params=pltpu.CompilerParams(vmem_limit_bytes=VMEM_LIMIT),
        cost_estimate=cost(0, 4096),
    )(x, *tokens)


def copied(x, token):
    def kernel(x_ref, token_ref, out_ref):
        out_ref[...] = x_ref[...]

    return pl.pallas_call(
        kernel,
        out_shape=jax.ShapeDtypeStruct(x.shape, x.dtype),
        in_specs=[VMEM] * 2,
        out_specs=VMEM,
        compiler_params=pltpu.CompilerParams(vmem_limit_bytes=VMEM_LIMIT),
        cost_estimate=cost(0, 2 * x.size * 2),
    )(x, token)


def part(x, unit):
    def kernel(x_ref, *refs):
        refs[-1][...] = x_ref[unit * UNIT : (unit + 1) * UNIT]

    return pl.pallas_call(
        kernel,
        out_shape=jax.ShapeDtypeStruct((UNIT, *x.shape[1:]), x.dtype),
        in_specs=[VMEM],
        out_specs=VMEM,
        compiler_params=pltpu.CompilerParams(vmem_limit_bytes=VMEM_LIMIT),
        cost_estimate=cost(0, 2 * x.size),
    )(x)


def spread(x, along):
    return [(along(x, 1), 1), (along(x, -1), 3), (along(x, 2), 2)]


def exchange_z(x, step):
    return move(x, lambda z, core, y, u: (z ^ 1 if core == step else 3 - z, core, y, u))


def shards(gradient, momentum, params, bands):
    rep, fsdp = lax.axis_index("rep"), lax.axis_index("fsdp")
    place = jnp.stack(
        [lax.shift_right_logical(rep, 1), lax.shift_right_logical(fsdp, 2), fsdp & 3, rep & 1]
    ).astype(jnp.int32)
    table = cosine_table()
    forward = split_table(np.kron(np.eye(WIDE // GROUP), table.T))
    inverse = split_table(np.kron(np.eye(WIDE // GROUP), table))
    by_layer = jnp.transpose(bands[0], (0, 1, 3, 2))
    gradient, momentum, params, forward, inverse, by_layer = (
        pltpu.with_memory_space_constraint(x, pltpu.HBM)
        for x in (gradient, momentum, params, forward, inverse, by_layer)
    )
    theirs, own_gradient, own_momentum, own_params, forward_here, inverse_here, by_layer = pick_theirs(
        place, by_layer, gradient, momentum, params, forward, inverse
    )
    received = swap(theirs)
    mine = pick_own(place, by_layer, own_gradient, own_momentum, forward_here)
    chips = chip_sums(mine, received)
    two_chips = [pair_sum(chip, exchange_z(chip, 0)) for chip in chips]
    everyone = [exchange_z(block, 1) for block in two_chips]
    updated = []
    for unit in range(UNITS):
        updated.append(decode(two_chips[unit], everyone[unit], own_params, inverse_here, unit, two_chips[unit + 1 :]))

    first = []
    for unit, block in enumerate(updated):
        first.append([(block, 0)] + spread(block, along_first))
    own = bring_together(place, first)

    new_momentum, tokens = None, []
    for unit in range(UNITS):
        new_momentum, token = keep_rest(
            place, by_layer, gradient, momentum, forward_here, inverse_here, unit, new_momentum, [own]
        )
        tokens.append(token)

    ahead, behind = along_second(own, 1), along_second(own, -1)
    whole, token = write_blocks(place, None, [(own, 0, 0, 0)])
    tokens.append(token)
    ahead, behind = after(ahead, *tokens), after(behind, *tokens)
    across = [along_second(part(ahead, 0), 1), along_second(part(behind, 1), -1)]
    items = [(ahead, 0, 1, 0), (behind, 0, 3, 0), (swap(ahead), 0, 1, 1), (swap(behind), 0, 3, 1)]
    whole, token = write_blocks(place, whole, items)
    items = [(swap(copied(own, token)), 0, 0, 1)]
    for unit, block in enumerate(across):
        block = after(block, token)
        items += [(block, unit * UNIT, 2, 0), (swap(block), unit * UNIT, 2, 1)]
    whole, _ = write_blocks(place, whole, items)
    return new_momentum, whole.reshape(LAYERS, 16 * ROWS_HERE, WIDTH)


def solution(mesh):
    in_specs = (
        P("rep", None, "fsdp", None),
        P("rep", None, "fsdp", None),
        P(None, "fsdp", None),
        P("rep", None, "fsdp", None, None),
    )
    out_specs = (P("rep", None, "fsdp", None), P())
    return jax.shard_map(shards, mesh=mesh, in_specs=in_specs, out_specs=out_specs, check_vma=False)
```

```python
import math

import jax
import jax.numpy as jnp
import numpy as np
from jax import lax
from jax.experimental import pallas as pl
from jax.experimental.pallas import tpu as pltpu
from jax.sharding import PartitionSpec as P

GROUP = 64
BANDS = 8
LAYERS = 4
ROWS_HERE = 8
WIDTH = 13824
HALF = WIDTH // 2
WIDE = 256
LANES = 128
REPS = 8
BLOCKS = WIDTH // GROUP
UNIT = 2
UNITS = LAYERS // UNIT

decay_rate = 0.9
step_size = 1.0
VMEM_LIMIT = 16 * 1024 * 1024
VMEM_FIRST = 16 * 1024 * 1024


def cosine_table():
    k = np.arange(GROUP, dtype=np.float64)
    n = np.arange(GROUP, dtype=np.float64)
    scale = np.where(k == 0, math.sqrt(1.0 / GROUP), math.sqrt(2.0 / GROUP))
    return scale[:, None] * np.cos(math.pi * (2.0 * n[None, :] + 1.0) * k[:, None] / (2.0 * GROUP))


def split_table(table):
    high = jnp.asarray(table, jnp.float32).astype(jnp.bfloat16)
    low = (jnp.asarray(table, jnp.float32) - high.astype(jnp.float32)).astype(jnp.bfloat16)
    return jnp.stack([high, low])


def dot3(x, table_ref):
    high = x.astype(jnp.bfloat16)
    low = (x - high.astype(jnp.float32)).astype(jnp.bfloat16)
    total = jnp.dot(high, table_ref[1], preferred_element_type=jnp.float32)
    total += jnp.dot(low, table_ref[0], preferred_element_type=jnp.float32)
    return total + jnp.dot(high, table_ref[0], preferred_element_type=jnp.float32)


def stacked(x):
    return jnp.concatenate([x[:, at : at + WIDE] for at in range(0, x.shape[1], WIDE)], axis=0)


def pick_tiles(bands_ref, side, layers, spectra):
    lane = lax.broadcasted_iota(jnp.int32, (ROWS_HERE, LANES), 1)
    upper = lax.shift_right_logical(lane, 6)
    bit = lax.shift_left(jnp.ones_like(lane), lax.bitwise_and(lax.shift_right_logical(lane, 3), 7))
    tiles = {}
    for i, layer in enumerate(layers):
        chosen = bands_ref[layer, side]
        for tile in range(HALF // LANES):
            index = upper + (2 * tile + jnp.where(side == 0, 0, LANES - BLOCKS // 2))
            here = jnp.take_along_axis(chosen, index, axis=1)
            row = (i * (HALF // WIDE) + tile // 2) * ROWS_HERE
            column = (tile % 2) * LANES
            values = spectra[row : row + ROWS_HERE, column : column + LANES]
            tiles[i, tile] = jnp.where(lax.bitwise_and(here, bit) != 0, values, 0.0)
    return tiles


def merged_rows(gradient, momentum):
    merged = decay_rate * momentum + gradient.astype(jnp.float32)
    return jnp.concatenate([stacked(merged[i]) for i in range(merged.shape[0])], axis=0)


HBM = pl.BlockSpec(memory_space=pl.ANY)
VMEM = pl.BlockSpec(memory_space=pltpu.VMEM)
SMEM = pl.BlockSpec(memory_space=pltpu.SMEM)
HALF_UNIT = jax.ShapeDtypeStruct((UNIT, ROWS_HERE, HALF), jnp.bfloat16)
HALF_LAYERS = jax.ShapeDtypeStruct((LAYERS, ROWS_HERE, HALF), jnp.bfloat16)
HALF_MOMENTUM = jax.ShapeDtypeStruct((LAYERS, ROWS_HERE, HALF), jnp.float32)
TABLE = jax.ShapeDtypeStruct((2, WIDE, WIDE), jnp.bfloat16)
SIDE_BANDS = jax.ShapeDtypeStruct((LAYERS, 2, ROWS_HERE, LANES), jnp.int32)
TOKEN = jax.ShapeDtypeStruct((8, 128), jnp.float32)


def cost(flops, size):
    return pl.CostEstimate(flops=flops, bytes_accessed=size, transcendentals=0)


def store_picked(bands_ref, side, unit, spectra, out_ref):
    layers = range(unit * UNIT, unit * UNIT + UNIT)
    for (layer, tile), values in pick_tiles(bands_ref, side, layers, spectra).items():
        out_ref[unit * UNIT + layer, :, tile * LANES : (tile + 1) * LANES] = values.astype(jnp.bfloat16)


def pick_theirs(place, by_layer, gradient, momentum, params, forward, inverse):
    out_shapes = [HALF_LAYERS, HALF_LAYERS, HALF_MOMENTUM, HALF_LAYERS, TABLE, TABLE, SIDE_BANDS]

    def kernel(place_ref, raw_ref, gradient_ref, momentum_ref, params_ref, forward_ref, inverse_ref, *refs):
        picked, own_gradient, own_momentum, own_params, table, back_table, bands_ref = refs[:7]
        gradients, momenta, raw, sems = refs[7:]
        core = place_ref[3]
        own = pl.ds(pl.multiple_of(core * HALF, LANES), HALF)
        theirs = pl.ds(pl.multiple_of((1 - core) * HALF, LANES), HALF)
        pairs = [(forward_ref, table)]
        for unit in range(UNITS):
            layers = pl.ds(unit * UNIT, UNIT)
            pairs.append((gradient_ref.at[0, layers, :, theirs], gradients.at[layers]))
            pairs.append((momentum_ref.at[0, layers, :, theirs], momenta.at[layers]))
        pairs.append((gradient_ref.at[0, :, :, own], own_gradient))
        pairs.append((momentum_ref.at[0, :, :, own], own_momentum))
        pairs.append((params_ref.at[:, :, own], own_params))
        pairs.append((inverse_ref, back_table))
        pairs.insert(0, (raw_ref, raw))
        copies = [pltpu.make_async_copy(src, dst, sems.at[i]) for i, (src, dst) in enumerate(pairs)]
        for copy in copies:
            copy.start()
        copies[0].wait()
        for layer in range(LAYERS):
            both = raw[layer]
            bits = lax.shift_left(jnp.ones_like(both), both)
            bits = lax.bitwise_or(bits[:, 0], bits[:, 1])
            bands_ref[layer, 0] = bits[:, :LANES]
            bands_ref[layer, 1] = bits[:, BLOCKS - LANES :]
        copies.pop(0)
        copies[0].wait()
        for unit in range(UNITS):
            copies[1 + 2 * unit].wait()
            copies[2 + 2 * unit].wait()
            layers = slice(unit * UNIT, unit * UNIT + UNIT)
            spectra = dot3(merged_rows(gradients[layers], momenta[layers]), table)
            store_picked(bands_ref, 1 - core, unit, spectra, picked)
        for copy in copies[1 + 2 * UNITS :]:
            copy.wait()

    return pl.pallas_call(
        kernel,
        out_shape=out_shapes,
        in_specs=[SMEM] + [HBM] * 6,
        out_specs=[VMEM] * len(out_shapes),
        scratch_shapes=[
            pltpu.VMEM((LAYERS, ROWS_HERE, HALF), jnp.bfloat16),
            pltpu.VMEM((LAYERS, ROWS_HERE, HALF), jnp.float32),
            pltpu.VMEM((LAYERS, ROWS_HERE, 2, BLOCKS), jnp.int32),
            pltpu.SemaphoreType.DMA((6 + 2 * UNITS,)),
        ],
        compiler_params=pltpu.CompilerParams(vmem_limit_bytes=VMEM_FIRST),
        cost_estimate=cost(6 * LAYERS * ROWS_HERE * HALF * WIDE, 6000000),
    )(place, by_layer, gradient, momentum, params, forward, inverse)


def pick_own(place, by_layer, gradient, momentum, forward):
    def kernel(place_ref, bands_ref, gradient_ref, momentum_ref, table_ref, picked):
        for unit in range(UNITS):
            layers = slice(unit * UNIT, unit * UNIT + UNIT)
            spectra = dot3(merged_rows(gradient_ref[layers], momentum_ref[layers]), table_ref)
            store_picked(bands_ref, place_ref[3], unit, spectra, picked)

    return pl.pallas_call(
        kernel,
        out_shape=HALF_LAYERS,
        in_specs=[SMEM] + [VMEM] * 4,
        out_specs=VMEM,
        compiler_params=pltpu.CompilerParams(vmem_limit_bytes=VMEM_LIMIT),
        cost_estimate=cost(6 * LAYERS * ROWS_HERE * HALF * WIDE, 2000000),
    )(place, by_layer, gradient, momentum, forward)


def chip_sums(mine, received):
    def kernel(mine_ref, received_ref, *outs):
        for unit, out_ref in enumerate(outs):
            layers = slice(unit * UNIT, (unit + 1) * UNIT)
            total = mine_ref[layers].astype(jnp.float32) + received_ref[layers].astype(jnp.float32)
            out_ref[...] = total.astype(jnp.bfloat16)

    return pl.pallas_call(
        kernel,
        out_shape=[HALF_UNIT] * UNITS,
        in_specs=[VMEM] * 2,
        out_specs=[VMEM] * UNITS,
        compiler_params=pltpu.CompilerParams(vmem_limit_bytes=VMEM_LIMIT),
        cost_estimate=cost(0, 1400000),
    )(mine, received)


def pair_sum(mine, received, tokens=()):
    def kernel(mine_ref, received_ref, *refs):
        total = mine_ref[...].astype(jnp.float32) + received_ref[...].astype(jnp.float32)
        refs[-1][...] = total.astype(jnp.bfloat16)

    return pl.pallas_call(
        kernel,
        out_shape=HALF_UNIT,
        in_specs=[VMEM] * (2 + len(tokens)),
        out_specs=VMEM,
        compiler_params=pltpu.CompilerParams(vmem_limit_bytes=VMEM_LIMIT),
        cost_estimate=cost(0, 700000),
    )(mine, received, *tokens)


def keep_rest(place, by_layer, gradient, momentum, forward, inverse, unit, before, tokens=()):
    def kernel(bands_ref, gradient_ref, momentum_ref, forward_ref, inverse_ref, *refs):
        out_ref, token_ref, gradients, momenta, table, sems = refs[-6:]
        token_ref[...] = jnp.zeros_like(token_ref)
        layers = pl.ds(unit * UNIT, UNIT)
        pairs = [(forward_ref, table)]
        for side in range(2):
            columns = pl.ds(side * HALF, HALF)
            pairs.append((gradient_ref.at[0, layers, :, columns], gradients.at[side]))
            pairs.append((momentum_ref.at[0, layers, :, columns], momenta.at[side]))
        copies = [pltpu.make_async_copy(src, dst, sems.at[i]) for i, (src, dst) in enumerate(pairs)]
        for copy in copies:
            copy.start()
        copies[0].wait()
        for side in range(2):
            copies[1 + 2 * side].wait()
            copies[2 + 2 * side].wait()
            merged = merged_rows(gradients[side], momenta[side])
            spectra = dot3(merged, table)
            tiles = pick_tiles(bands_ref, side, range(unit * UNIT, unit * UNIT + UNIT), spectra)
            wide = [
                jnp.concatenate([tiles[i, at], tiles[i, at + 1]], axis=1)
                for i in range(UNIT)
                for at in range(0, HALF // LANES, 2)
            ]
            kept = merged - dot3(jnp.concatenate(wide, axis=0), inverse_ref)
            for i in range(UNIT):
                for at in range(HALF // WIDE):
                    row = (i * (HALF // WIDE) + at) * ROWS_HERE
                    momenta[side, i, :, at * WIDE : (at + 1) * WIDE] = kept[row : row + ROWS_HERE]
            target = out_ref.at[0, layers, :, pl.ds(side * HALF, HALF)]
            copies.append(pltpu.make_async_copy(momenta.at[side], target, sems.at[5 + side]))
            copies[-1].start()
        copies[-2].wait()
        copies[-1].wait()

    operands = [by_layer, gradient, momentum, forward, inverse, *tokens]
    specs = [VMEM, HBM, HBM, HBM, VMEM] + [VMEM] * len(tokens)
    aliases = {}
    if before is not None:
        aliases = {len(operands): 0}
        operands.append(before)
        specs.append(HBM)
    return pl.pallas_call(
        kernel,
        out_shape=[jax.ShapeDtypeStruct(momentum.shape, jnp.float32), TOKEN],
        in_specs=specs,
        out_specs=[HBM, VMEM],
        scratch_shapes=[
            pltpu.VMEM((2, UNIT, ROWS_HERE, HALF), jnp.bfloat16),
            pltpu.VMEM((2, UNIT, ROWS_HERE, HALF), jnp.float32),
            pltpu.VMEM((2, WIDE, WIDE), jnp.bfloat16),
            pltpu.SemaphoreType.DMA((7,)),
        ],
        input_output_aliases=aliases,
        compiler_params=pltpu.CompilerParams(vmem_limit_bytes=VMEM_LIMIT),
        cost_estimate=cost(12 * UNIT * ROWS_HERE * WIDTH * WIDE, 3000000),
    )(*operands)


def decode(mine, received, params, inverse, unit, tokens=()):
    def kernel(mine_ref, received_ref, params_ref, inverse_ref, *refs):
        total = mine_ref[...].astype(jnp.float32) + received_ref[...].astype(jnp.float32)
        total = total * (1.0 / REPS)
        restored = jnp.concatenate([stacked(total[i]) for i in range(UNIT)], axis=0)
        decoded = dot3(restored, inverse_ref)
        for i in range(UNIT):
            for at in range(HALF // WIDE):
                columns = slice(at * WIDE, (at + 1) * WIDE)
                row = (i * (HALF // WIDE) + at) * ROWS_HERE
                change = step_size * decoded[row : row + ROWS_HERE]
                updated = params_ref[unit * UNIT + i, :, columns].astype(jnp.float32) - change
                refs[-1][i, :, columns] = updated.astype(jnp.bfloat16)

    return pl.pallas_call(
        kernel,
        out_shape=HALF_UNIT,
        in_specs=[VMEM] * (4 + len(tokens)),
        out_specs=VMEM,
        compiler_params=pltpu.CompilerParams(vmem_limit_bytes=VMEM_LIMIT),
        cost_estimate=cost(6 * UNIT * ROWS_HERE * HALF * WIDE, 1500000),
    )(mine, received, params, inverse, *tokens)


def first_place(place_ref):
    return jnp.where(place_ref[3] == 0, place_ref[2], place_ref[1])


def second_place(place_ref):
    return jnp.where(place_ref[3] == 0, place_ref[1], place_ref[2])


def bring_together(place, units):
    blocks = [block for unit in units for block, _ in unit]

    def kernel(place_ref, *refs):
        here = first_place(place_ref)
        ins = iter(refs)
        for at, unit in enumerate(units):
            for _, steps in unit:
                refs[-1][at * UNIT : (at + 1) * UNIT, lax.rem(here + (4 - steps), 4)] = next(ins)[...]

    return pl.pallas_call(
        kernel,
        out_shape=jax.ShapeDtypeStruct((LAYERS, 4, ROWS_HERE, HALF), jnp.bfloat16),
        in_specs=[SMEM] + [VMEM] * len(blocks),
        out_specs=VMEM,
        compiler_params=pltpu.CompilerParams(vmem_limit_bytes=VMEM_LIMIT),
        cost_estimate=cost(0, 3600000),
    )(place, *blocks)


def write_blocks(place, whole, items):
    blocks = [item[0] for item in items]

    def kernel(place_ref, *refs):
        ins, (out, token_ref, sems) = refs[: len(blocks)], refs[-3:]
        token_ref[...] = jnp.zeros_like(token_ref)
        y, x, core = place_ref[1], place_ref[2], place_ref[3]
        copies = []
        for block, (_, first_layer, steps, other) in zip(ins, items):
            side = core if other == 0 else 1 - core
            columns = pl.ds(pl.multiple_of(side * HALF, LANES), HALF)
            along, across = jnp.where(side == 0, x, y), jnp.where(side == 0, y, x)
            if len(block.shape) == 4:
                across = lax.rem(across + (4 - steps), 4)
                parts = [(i, layer, block.at[layer, i]) for i in range(4) for layer in range(block.shape[0])]
            else:
                along = lax.rem(along + (4 - steps), 4)
                parts = [(along, layer, block.at[layer]) for layer in range(block.shape[0])]
            for i, layer, source in parts:
                rows = jnp.where(side == 0, 4 * across + i, 4 * i + across)
                target = out.at[first_layer + layer, rows, :, columns]
                copies.append(pltpu.make_async_copy(source, target, sems.at[len(copies)]))
        for copy in copies:
            copy.start()
        for copy in copies:
            copy.wait()

    operands = [place] + blocks
    specs = [SMEM] + [VMEM] * len(blocks)
    aliases = {}
    if whole is not None:
        aliases = {len(operands): 0}
        operands.append(whole)
        specs.append(HBM)
    return pl.pallas_call(
        kernel,
        out_shape=[jax.ShapeDtypeStruct((LAYERS, 16, ROWS_HERE, WIDTH), jnp.bfloat16), TOKEN],
        in_specs=specs,
        out_specs=[HBM, VMEM],
        scratch_shapes=[pltpu.SemaphoreType.DMA((4 * sum(block.shape[0] for block in blocks),))],
        input_output_aliases=aliases,
        compiler_params=pltpu.CompilerParams(vmem_limit_bytes=VMEM_LIMIT),
        cost_estimate=cost(0, 2 * sum(b.size * 2 for b in blocks)),
    )(*operands)


def move(x, step):
    pairs = []
    for device in range(128):
        z, core, y, u = device // 32, device // 16 % 2, device // 4 % 4, device % 4
        z, core, y, u = step(z, core, y, u)
        pairs.append((device, (z % 4 * 2 + core) * 16 + y % 4 * 4 + u % 4))
    return lax.ppermute(x, ("rep", "fsdp"), pairs)


def swap(x):
    return move(x, lambda z, core, y, u: (z, 1 - core, y, u))


def along_first(x, by):
    return move(x, lambda z, core, y, u: (z, core, y, u + by) if core == 0 else (z, core, y + by, u))


def along_second(x, by):
    return move(x, lambda z, core, y, u: (z, core, y + by, u) if core == 0 else (z, core, y, u + by))


def after(x, *tokens):
    def kernel(x_ref, *refs):
        pass

    return pl.pallas_call(
        kernel,
        out_shape=jax.ShapeDtypeStruct(x.shape, x.dtype),
        in_specs=[VMEM] * (1 + len(tokens)),
        out_specs=VMEM,
        input_output_aliases={0: 0},
        compiler_params=pltpu.CompilerParams(vmem_limit_bytes=VMEM_LIMIT),
        cost_estimate=cost(0, 4096),
    )(x, *tokens)


def copied(x, token):
    def kernel(x_ref, token_ref, out_ref):
        out_ref[...] = x_ref[...]

    return pl.pallas_call(
        kernel,
        out_shape=jax.ShapeDtypeStruct(x.shape, x.dtype),
        in_specs=[VMEM] * 2,
        out_specs=VMEM,
        compiler_params=pltpu.CompilerParams(vmem_limit_bytes=VMEM_LIMIT),
        cost_estimate=cost(0, 2 * x.size * 2),
    )(x, token)


def part(x, unit):
    def kernel(x_ref, *refs):
        refs[-1][...] = x_ref[unit * UNIT : (unit + 1) * UNIT]

    return pl.pallas_call(
        kernel,
        out_shape=jax.ShapeDtypeStruct((UNIT, *x.shape[1:]), x.dtype),
        in_specs=[VMEM],
        out_specs=VMEM,
        compiler_params=pltpu.CompilerParams(vmem_limit_bytes=VMEM_LIMIT),
        cost_estimate=cost(0, 2 * x.size),
    )(x)


def spread(x, along):
    return [(along(x, 1), 1), (along(x, -1), 3), (along(x, 2), 2)]


def exchange_z(x, step):
    return move(x, lambda z, core, y, u: (z ^ 1 if core == step else 3 - z, core, y, u))


def shards(gradient, momentum, params, bands):
    rep, fsdp = lax.axis_index("rep"), lax.axis_index("fsdp")
    place = jnp.stack(
        [lax.shift_right_logical(rep, 1), lax.shift_right_logical(fsdp, 2), fsdp & 3, rep & 1]
    ).astype(jnp.int32)
    table = cosine_table()
    forward = split_table(np.kron(np.eye(WIDE // GROUP), table.T))
    inverse = split_table(np.kron(np.eye(WIDE // GROUP), table))
    by_layer = jnp.transpose(bands[0], (0, 1, 3, 2))
    gradient, momentum, params, forward, inverse, by_layer = (
        pltpu.with_memory_space_constraint(x, pltpu.HBM)
        for x in (gradient, momentum, params, forward, inverse, by_layer)
    )
    theirs, own_gradient, own_momentum, own_params, forward_here, inverse_here, by_layer = pick_theirs(
        place, by_layer, gradient, momentum, params, forward, inverse
    )
    received = swap(theirs)
    mine = pick_own(place, by_layer, own_gradient, own_momentum, forward_here)
    chips = chip_sums(mine, received)
    two_chips = [pair_sum(chip, exchange_z(chip, 0)) for chip in chips]
    everyone = [exchange_z(block, 1) for block in two_chips]
    updated = []
    for unit in range(UNITS):
        updated.append(decode(two_chips[unit], everyone[unit], own_params, inverse_here, unit, two_chips[unit + 1 :]))

    first = []
    for unit, block in enumerate(updated):
        first.append([(block, 0)] + spread(block, along_first))
    own = bring_together(place, first)

    new_momentum, tokens = None, []
    for unit in range(UNITS):
        new_momentum, token = keep_rest(
            place, by_layer, gradient, momentum, forward_here, inverse_here, unit, new_momentum, [own]
        )
        tokens.append(token)

    ahead, behind = along_second(own, 1), along_second(own, -1)
    items = [(own, 0, 0, 0)]
    for unit, blocks in enumerate(first):
        items += [(swap(block), unit * UNIT, steps, 1) for block, steps in blocks]
    whole, token = write_blocks(place, None, items)
    tokens.append(token)
    ahead, behind = after(ahead, *tokens), after(behind, *tokens)
    across = [along_second(part(behind, 0), -1), along_second(part(ahead, 1), 1)]
    items = [(ahead, 0, 1, 0), (behind, 0, 3, 0)]
    for unit in range(UNITS):
        items += [(swap(part(block, unit)), unit * UNIT, steps, 1) for block, steps in ((ahead, 1), (behind, 3))]
    whole, token = write_blocks(place, whole, items)
    across = [after(block, token) for block in across]
    others = [swap(block) for block in across]
    for other, blocks in enumerate((across, others)):
        whole, _ = write_blocks(place, whole, [(block, unit * UNIT, 2, other) for unit, block in enumerate(blocks)])
    return new_momentum, whole.reshape(LAYERS, 16 * ROWS_HERE, WIDTH)


def solution(mesh):
    in_specs = (
        P("rep", None, "fsdp", None),
        P("rep", None, "fsdp", None),
        P(None, "fsdp", None),
        P("rep", None, "fsdp", None, None),
    )
    out_specs = (P("rep", None, "fsdp", None), P())
    return jax.shard_map(shards, mesh=mesh, in_specs=in_specs, out_specs=out_specs, check_vma=False)
```

```python
import math

import jax
import jax.numpy as jnp
import numpy as np
from jax import lax
from jax.experimental import pallas as pl
from jax.experimental.pallas import tpu as pltpu
from jax.sharding import PartitionSpec as P

GROUP = 64
BANDS = 8
LAYERS = 4
ROWS_HERE = 8
WIDTH = 13824
HALF = WIDTH // 2
WIDE = 256
LANES = 128
REPS = 8
BLOCKS = WIDTH // GROUP
UNIT = 2
UNITS = LAYERS // UNIT

decay_rate = 0.9
step_size = 1.0
VMEM_LIMIT = 16 * 1024 * 1024
VMEM_FIRST = 16 * 1024 * 1024


def cosine_table():
    k = np.arange(GROUP, dtype=np.float64)
    n = np.arange(GROUP, dtype=np.float64)
    scale = np.where(k == 0, math.sqrt(1.0 / GROUP), math.sqrt(2.0 / GROUP))
    return scale[:, None] * np.cos(math.pi * (2.0 * n[None, :] + 1.0) * k[:, None] / (2.0 * GROUP))


def split_table(table):
    high = jnp.asarray(table, jnp.float32).astype(jnp.bfloat16)
    low = (jnp.asarray(table, jnp.float32) - high.astype(jnp.float32)).astype(jnp.bfloat16)
    return jnp.stack([high, low])


def dot3(x, table_ref):
    high = x.astype(jnp.bfloat16)
    low = (x - high.astype(jnp.float32)).astype(jnp.bfloat16)
    total = jnp.dot(high, table_ref[1], preferred_element_type=jnp.float32)
    total += jnp.dot(low, table_ref[0], preferred_element_type=jnp.float32)
    return total + jnp.dot(high, table_ref[0], preferred_element_type=jnp.float32)


def stacked(x):
    return jnp.concatenate([x[:, at : at + WIDE] for at in range(0, x.shape[1], WIDE)], axis=0)


def pick_tiles(bands_ref, side, layers, spectra):
    lane = lax.broadcasted_iota(jnp.int32, (ROWS_HERE, LANES), 1)
    upper = lax.shift_right_logical(lane, 6)
    bit = lax.shift_left(jnp.ones_like(lane), lax.bitwise_and(lax.shift_right_logical(lane, 3), 7))
    tiles = {}
    for i, layer in enumerate(layers):
        chosen = bands_ref[layer, side]
        for tile in range(HALF // LANES):
            index = upper + (2 * tile + jnp.where(side == 0, 0, LANES - BLOCKS // 2))
            here = jnp.take_along_axis(chosen, index, axis=1)
            row = (i * (HALF // WIDE) + tile // 2) * ROWS_HERE
            column = (tile % 2) * LANES
            values = spectra[row : row + ROWS_HERE, column : column + LANES]
            tiles[i, tile] = jnp.where(lax.bitwise_and(here, bit) != 0, values, 0.0)
    return tiles


def merged_rows(gradient, momentum):
    merged = decay_rate * momentum + gradient.astype(jnp.float32)
    return jnp.concatenate([stacked(merged[i]) for i in range(merged.shape[0])], axis=0)


HBM = pl.BlockSpec(memory_space=pl.ANY)
VMEM = pl.BlockSpec(memory_space=pltpu.VMEM)
SMEM = pl.BlockSpec(memory_space=pltpu.SMEM)
HALF_UNIT = jax.ShapeDtypeStruct((UNIT, ROWS_HERE, HALF), jnp.bfloat16)
HALF_LAYERS = jax.ShapeDtypeStruct((LAYERS, ROWS_HERE, HALF), jnp.bfloat16)
HALF_MOMENTUM = jax.ShapeDtypeStruct((LAYERS, ROWS_HERE, HALF), jnp.float32)
TABLE = jax.ShapeDtypeStruct((2, WIDE, WIDE), jnp.bfloat16)
SIDE_BANDS = jax.ShapeDtypeStruct((LAYERS, 2, ROWS_HERE, LANES), jnp.int32)
TOKEN = jax.ShapeDtypeStruct((8, 128), jnp.float32)


def cost(flops, size):
    return pl.CostEstimate(flops=flops, bytes_accessed=size, transcendentals=0)


def store_picked(bands_ref, side, unit, spectra, out_ref):
    layers = range(unit * UNIT, unit * UNIT + UNIT)
    for (layer, tile), values in pick_tiles(bands_ref, side, layers, spectra).items():
        out_ref[unit * UNIT + layer, :, tile * LANES : (tile + 1) * LANES] = values.astype(jnp.bfloat16)


def pick_theirs(place, by_layer, gradient, momentum, forward):
    out_shapes = [HALF_LAYERS, HALF_LAYERS, HALF_MOMENTUM, TABLE, SIDE_BANDS]

    def kernel(place_ref, raw_ref, gradient_ref, momentum_ref, forward_ref, *refs):
        picked, own_gradient, own_momentum, table, bands_ref = refs[:5]
        gradients, momenta, raw, sems = refs[5:]
        core = place_ref[3]
        own = pl.ds(pl.multiple_of(core * HALF, LANES), HALF)
        theirs = pl.ds(pl.multiple_of((1 - core) * HALF, LANES), HALF)
        pairs = [(forward_ref, table)]
        for unit in range(UNITS):
            layers = pl.ds(unit * UNIT, UNIT)
            pairs.append((gradient_ref.at[0, layers, :, theirs], gradients.at[layers]))
            pairs.append((momentum_ref.at[0, layers, :, theirs], momenta.at[layers]))
        pairs.append((gradient_ref.at[0, :, :, own], own_gradient))
        pairs.append((momentum_ref.at[0, :, :, own], own_momentum))
        pairs.insert(0, (raw_ref, raw))
        copies = [pltpu.make_async_copy(src, dst, sems.at[i]) for i, (src, dst) in enumerate(pairs)]
        for copy in copies:
            copy.start()
        copies[0].wait()
        for layer in range(LAYERS):
            both = raw[layer]
            bits = lax.shift_left(jnp.ones_like(both), both)
            bits = lax.bitwise_or(bits[:, 0], bits[:, 1])
            bands_ref[layer, 0] = bits[:, :LANES]
            bands_ref[layer, 1] = bits[:, BLOCKS - LANES :]
        copies.pop(0)
        copies[0].wait()
        for unit in range(UNITS):
            copies[1 + 2 * unit].wait()
            copies[2 + 2 * unit].wait()
            layers = slice(unit * UNIT, unit * UNIT + UNIT)
            spectra = dot3(merged_rows(gradients[layers], momenta[layers]), table)
            store_picked(bands_ref, 1 - core, unit, spectra, picked)
        for copy in copies[1 + 2 * UNITS :]:
            copy.wait()

    return pl.pallas_call(
        kernel,
        out_shape=out_shapes,
        in_specs=[SMEM] + [HBM] * 4,
        out_specs=[VMEM] * len(out_shapes),
        scratch_shapes=[
            pltpu.VMEM((LAYERS, ROWS_HERE, HALF), jnp.bfloat16),
            pltpu.VMEM((LAYERS, ROWS_HERE, HALF), jnp.float32),
            pltpu.VMEM((LAYERS, ROWS_HERE, 2, BLOCKS), jnp.int32),
            pltpu.SemaphoreType.DMA((4 + 2 * UNITS,)),
        ],
        compiler_params=pltpu.CompilerParams(vmem_limit_bytes=VMEM_FIRST),
        cost_estimate=cost(6 * LAYERS * ROWS_HERE * HALF * WIDE, 6000000),
    )(place, by_layer, gradient, momentum, forward)


def pick_own(place, by_layer, gradient, momentum, forward, params, inverse):
    def kernel(place_ref, bands_ref, gradient_ref, momentum_ref, table_ref, params_ref, inverse_ref, *refs):
        picked, own_params, back_table, sems = refs
        own = pl.ds(pl.multiple_of(place_ref[3] * HALF, LANES), HALF)
        copies = [
            pltpu.make_async_copy(params_ref.at[:, :, own], own_params, sems.at[0]),
            pltpu.make_async_copy(inverse_ref, back_table, sems.at[1]),
        ]
        for copy in copies:
            copy.start()
        for unit in range(UNITS):
            layers = slice(unit * UNIT, unit * UNIT + UNIT)
            spectra = dot3(merged_rows(gradient_ref[layers], momentum_ref[layers]), table_ref)
            store_picked(bands_ref, place_ref[3], unit, spectra, picked)
        for copy in copies:
            copy.wait()

    return pl.pallas_call(
        kernel,
        out_shape=[HALF_LAYERS, HALF_LAYERS, TABLE],
        in_specs=[SMEM] + [VMEM] * 4 + [HBM] * 2,
        out_specs=[VMEM] * 3,
        scratch_shapes=[pltpu.SemaphoreType.DMA((2,))],
        compiler_params=pltpu.CompilerParams(vmem_limit_bytes=VMEM_LIMIT),
        cost_estimate=cost(6 * LAYERS * ROWS_HERE * HALF * WIDE, 2000000),
    )(place, by_layer, gradient, momentum, forward, params, inverse)


def chip_sums(mine, received):
    def kernel(mine_ref, received_ref, *outs):
        for unit, out_ref in enumerate(outs):
            layers = slice(unit * UNIT, (unit + 1) * UNIT)
            total = mine_ref[layers].astype(jnp.float32) + received_ref[layers].astype(jnp.float32)
            out_ref[...] = total.astype(jnp.bfloat16)

    return pl.pallas_call(
        kernel,
        out_shape=[HALF_UNIT] * UNITS,
        in_specs=[VMEM] * 2,
        out_specs=[VMEM] * UNITS,
        compiler_params=pltpu.CompilerParams(vmem_limit_bytes=VMEM_LIMIT),
        cost_estimate=cost(0, 1400000),
    )(mine, received)


def pair_sum(mine, received, tokens=()):
    def kernel(mine_ref, received_ref, *refs):
        total = mine_ref[...].astype(jnp.float32) + received_ref[...].astype(jnp.float32)
        refs[-1][...] = total.astype(jnp.bfloat16)

    return pl.pallas_call(
        kernel,
        out_shape=HALF_UNIT,
        in_specs=[VMEM] * (2 + len(tokens)),
        out_specs=VMEM,
        compiler_params=pltpu.CompilerParams(vmem_limit_bytes=VMEM_LIMIT),
        cost_estimate=cost(0, 700000),
    )(mine, received, *tokens)


def keep_rest(place, by_layer, gradient, momentum, forward, inverse, unit, before, tokens=()):
    def kernel(bands_ref, gradient_ref, momentum_ref, forward_ref, inverse_ref, *refs):
        out_ref, token_ref, gradients, momenta, table, sems = refs[-6:]
        token_ref[...] = jnp.zeros_like(token_ref)
        layers = pl.ds(unit * UNIT, UNIT)
        pairs = [(forward_ref, table)]
        for side in range(2):
            columns = pl.ds(side * HALF, HALF)
            pairs.append((gradient_ref.at[0, layers, :, columns], gradients.at[side]))
            pairs.append((momentum_ref.at[0, layers, :, columns], momenta.at[side]))
        copies = [pltpu.make_async_copy(src, dst, sems.at[i]) for i, (src, dst) in enumerate(pairs)]
        for copy in copies:
            copy.start()
        copies[0].wait()
        for side in range(2):
            copies[1 + 2 * side].wait()
            copies[2 + 2 * side].wait()
            merged = merged_rows(gradients[side], momenta[side])
            spectra = dot3(merged, table)
            tiles = pick_tiles(bands_ref, side, range(unit * UNIT, unit * UNIT + UNIT), spectra)
            wide = [
                jnp.concatenate([tiles[i, at], tiles[i, at + 1]], axis=1)
                for i in range(UNIT)
                for at in range(0, HALF // LANES, 2)
            ]
            kept = merged - dot3(jnp.concatenate(wide, axis=0), inverse_ref)
            for i in range(UNIT):
                for at in range(HALF // WIDE):
                    row = (i * (HALF // WIDE) + at) * ROWS_HERE
                    momenta[side, i, :, at * WIDE : (at + 1) * WIDE] = kept[row : row + ROWS_HERE]
            target = out_ref.at[0, layers, :, pl.ds(side * HALF, HALF)]
            copies.append(pltpu.make_async_copy(momenta.at[side], target, sems.at[5 + side]))
            copies[-1].start()
        copies[-2].wait()
        copies[-1].wait()

    operands = [by_layer, gradient, momentum, forward, inverse, *tokens]
    specs = [VMEM, HBM, HBM, HBM, VMEM] + [VMEM] * len(tokens)
    aliases = {}
    if before is not None:
        aliases = {len(operands): 0}
        operands.append(before)
        specs.append(HBM)
    return pl.pallas_call(
        kernel,
        out_shape=[jax.ShapeDtypeStruct(momentum.shape, jnp.float32), TOKEN],
        in_specs=specs,
        out_specs=[HBM, VMEM],
        scratch_shapes=[
            pltpu.VMEM((2, UNIT, ROWS_HERE, HALF), jnp.bfloat16),
            pltpu.VMEM((2, UNIT, ROWS_HERE, HALF), jnp.float32),
            pltpu.VMEM((2, WIDE, WIDE), jnp.bfloat16),
            pltpu.SemaphoreType.DMA((7,)),
        ],
        input_output_aliases=aliases,
        compiler_params=pltpu.CompilerParams(vmem_limit_bytes=VMEM_LIMIT),
        cost_estimate=cost(12 * UNIT * ROWS_HERE * WIDTH * WIDE, 3000000),
    )(*operands)


def decode(mine, received, params, inverse, unit, tokens=()):
    def kernel(mine_ref, received_ref, params_ref, inverse_ref, *refs):
        total = mine_ref[...].astype(jnp.float32) + received_ref[...].astype(jnp.float32)
        total = total * (1.0 / REPS)
        restored = jnp.concatenate([stacked(total[i]) for i in range(UNIT)], axis=0)
        decoded = dot3(restored, inverse_ref)
        for i in range(UNIT):
            for at in range(HALF // WIDE):
                columns = slice(at * WIDE, (at + 1) * WIDE)
                row = (i * (HALF // WIDE) + at) * ROWS_HERE
                change = step_size * decoded[row : row + ROWS_HERE]
                updated = params_ref[unit * UNIT + i, :, columns].astype(jnp.float32) - change
                refs[-1][i, :, columns] = updated.astype(jnp.bfloat16)

    return pl.pallas_call(
        kernel,
        out_shape=HALF_UNIT,
        in_specs=[VMEM] * (4 + len(tokens)),
        out_specs=VMEM,
        compiler_params=pltpu.CompilerParams(vmem_limit_bytes=VMEM_LIMIT),
        cost_estimate=cost(6 * UNIT * ROWS_HERE * HALF * WIDE, 1500000),
    )(mine, received, params, inverse, *tokens)


def first_place(place_ref):
    return jnp.where(place_ref[3] == 0, place_ref[2], place_ref[1])


def second_place(place_ref):
    return jnp.where(place_ref[3] == 0, place_ref[1], place_ref[2])


def bring_together(place, units):
    blocks = [block for unit in units for block, _ in unit]

    def kernel(place_ref, *refs):
        here = first_place(place_ref)
        ins = iter(refs)
        for at, unit in enumerate(units):
            for _, steps in unit:
                refs[-1][at * UNIT : (at + 1) * UNIT, lax.rem(here + (4 - steps), 4)] = next(ins)[...]

    return pl.pallas_call(
        kernel,
        out_shape=jax.ShapeDtypeStruct((LAYERS, 4, ROWS_HERE, HALF), jnp.bfloat16),
        in_specs=[SMEM] + [VMEM] * len(blocks),
        out_specs=VMEM,
        compiler_params=pltpu.CompilerParams(vmem_limit_bytes=VMEM_LIMIT),
        cost_estimate=cost(0, 3600000),
    )(place, *blocks)


def write_blocks(place, whole, items):
    blocks = [item[0] for item in items]

    def kernel(place_ref, *refs):
        ins, (out, token_ref, sems) = refs[: len(blocks)], refs[-3:]
        token_ref[...] = jnp.zeros_like(token_ref)
        y, x, core = place_ref[1], place_ref[2], place_ref[3]
        copies = []
        for block, (_, first_layer, steps, other) in zip(ins, items):
            side = core if other == 0 else 1 - core
            columns = pl.ds(pl.multiple_of(side * HALF, LANES), HALF)
            along, across = jnp.where(side == 0, x, y), jnp.where(side == 0, y, x)
            if len(block.shape) == 4:
                across = lax.rem(across + (4 - steps), 4)
                parts = [(i, layer, block.at[layer, i]) for i in range(4) for layer in range(block.shape[0])]
            else:
                along = lax.rem(along + (4 - steps), 4)
                parts = [(along, layer, block.at[layer]) for layer in range(block.shape[0])]
            for i, layer, source in parts:
                rows = jnp.where(side == 0, 4 * across + i, 4 * i + across)
                target = out.at[first_layer + layer, rows, :, columns]
                copies.append(pltpu.make_async_copy(source, target, sems.at[len(copies)]))
        for copy in copies:
            copy.start()
        for copy in copies:
            copy.wait()

    operands = [place] + blocks
    specs = [SMEM] + [VMEM] * len(blocks)
    aliases = {}
    if whole is not None:
        aliases = {len(operands): 0}
        operands.append(whole)
        specs.append(HBM)
    return pl.pallas_call(
        kernel,
        out_shape=[jax.ShapeDtypeStruct((LAYERS, 16, ROWS_HERE, WIDTH), jnp.bfloat16), TOKEN],
        in_specs=specs,
        out_specs=[HBM, VMEM],
        scratch_shapes=[pltpu.SemaphoreType.DMA((4 * sum(block.shape[0] for block in blocks),))],
        input_output_aliases=aliases,
        compiler_params=pltpu.CompilerParams(vmem_limit_bytes=VMEM_LIMIT),
        cost_estimate=cost(0, 2 * sum(b.size * 2 for b in blocks)),
    )(*operands)


def move(x, step):
    pairs = []
    for device in range(128):
        z, core, y, u = device // 32, device // 16 % 2, device // 4 % 4, device % 4
        z, core, y, u = step(z, core, y, u)
        pairs.append((device, (z % 4 * 2 + core) * 16 + y % 4 * 4 + u % 4))
    return lax.ppermute(x, ("rep", "fsdp"), pairs)


def swap(x):
    return move(x, lambda z, core, y, u: (z, 1 - core, y, u))


def along_first(x, by):
    return move(x, lambda z, core, y, u: (z, core, y, u + by) if core == 0 else (z, core, y + by, u))


def along_second(x, by):
    return move(x, lambda z, core, y, u: (z, core, y + by, u) if core == 0 else (z, core, y, u + by))


def after(x, *tokens):
    def kernel(x_ref, *refs):
        pass

    return pl.pallas_call(
        kernel,
        out_shape=jax.ShapeDtypeStruct(x.shape, x.dtype),
        in_specs=[VMEM] * (1 + len(tokens)),
        out_specs=VMEM,
        input_output_aliases={0: 0},
        compiler_params=pltpu.CompilerParams(vmem_limit_bytes=VMEM_LIMIT),
        cost_estimate=cost(0, 4096),
    )(x, *tokens)


def copied(x, token):
    def kernel(x_ref, token_ref, out_ref):
        out_ref[...] = x_ref[...]

    return pl.pallas_call(
        kernel,
        out_shape=jax.ShapeDtypeStruct(x.shape, x.dtype),
        in_specs=[VMEM] * 2,
        out_specs=VMEM,
        compiler_params=pltpu.CompilerParams(vmem_limit_bytes=VMEM_LIMIT),
        cost_estimate=cost(0, 2 * x.size * 2),
    )(x, token)


def part(x, unit):
    def kernel(x_ref, *refs):
        refs[-1][...] = x_ref[unit * UNIT : (unit + 1) * UNIT]

    return pl.pallas_call(
        kernel,
        out_shape=jax.ShapeDtypeStruct((UNIT, *x.shape[1:]), x.dtype),
        in_specs=[VMEM],
        out_specs=VMEM,
        compiler_params=pltpu.CompilerParams(vmem_limit_bytes=VMEM_LIMIT),
        cost_estimate=cost(0, 2 * x.size),
    )(x)


def spread(x, along):
    return [(along(x, 1), 1), (along(x, -1), 3), (along(x, 2), 2)]


def exchange_z(x, step):
    return move(x, lambda z, core, y, u: (z ^ 1 if core == step else 3 - z, core, y, u))


def shards(gradient, momentum, params, bands):
    rep, fsdp = lax.axis_index("rep"), lax.axis_index("fsdp")
    place = jnp.stack(
        [lax.shift_right_logical(rep, 1), lax.shift_right_logical(fsdp, 2), fsdp & 3, rep & 1]
    ).astype(jnp.int32)
    table = cosine_table()
    forward = split_table(np.kron(np.eye(WIDE // GROUP), table.T))
    inverse = split_table(np.kron(np.eye(WIDE // GROUP), table))
    by_layer = jnp.transpose(bands[0], (0, 1, 3, 2))
    gradient, momentum, params, forward, inverse, by_layer = (
        pltpu.with_memory_space_constraint(x, pltpu.HBM)
        for x in (gradient, momentum, params, forward, inverse, by_layer)
    )
    theirs, own_gradient, own_momentum, forward_here, by_layer = pick_theirs(
        place, by_layer, gradient, momentum, forward
    )
    received = swap(theirs)
    mine, own_params, inverse_here = pick_own(
        place, by_layer, own_gradient, own_momentum, forward_here, params, inverse
    )
    chips = chip_sums(mine, received)
    two_chips = [pair_sum(chip, exchange_z(chip, 0)) for chip in chips]
    everyone = [exchange_z(block, 1) for block in two_chips]
    updated = []
    for unit in range(UNITS):
        updated.append(decode(two_chips[unit], everyone[unit], own_params, inverse_here, unit, two_chips[unit + 1 :]))

    first = []
    for unit, block in enumerate(updated):
        first.append([(block, 0)] + spread(block, along_first))
    own = bring_together(place, first)

    new_momentum, tokens = None, []
    for unit in range(UNITS):
        new_momentum, token = keep_rest(
            place, by_layer, gradient, momentum, forward_here, inverse_here, unit, new_momentum, [own]
        )
        tokens.append(token)

    ahead, behind = along_second(own, 1), along_second(own, -1)
    items = [(own, 0, 0, 0)]
    for unit, blocks in enumerate(first):
        items += [(swap(block), unit * UNIT, steps, 1) for block, steps in blocks]
    whole, token = write_blocks(place, None, items)
    tokens.append(token)
    ahead, behind = after(ahead, *tokens), after(behind, *tokens)
    across = [along_second(part(behind, 0), -1), along_second(part(ahead, 1), 1)]
    items = [(ahead, 0, 1, 0), (behind, 0, 3, 0)]
    for unit in range(UNITS):
        items += [(swap(part(block, unit)), unit * UNIT, steps, 1) for block, steps in ((ahead, 1), (behind, 3))]
    whole, token = write_blocks(place, whole, items)
    across = [after(block, token) for block in across]
    others = [swap(block) for block in across]
    for other, blocks in enumerate((across, others)):
        whole, _ = write_blocks(place, whole, [(block, unit * UNIT, 2, other) for unit, block in enumerate(blocks)])
    return new_momentum, whole.reshape(LAYERS, 16 * ROWS_HERE, WIDTH)


def solution(mesh):
    in_specs = (
        P("rep", None, "fsdp", None),
        P("rep", None, "fsdp", None),
        P(None, "fsdp", None),
        P("rep", None, "fsdp", None, None),
    )
    out_specs = (P("rep", None, "fsdp", None), P())
    return jax.shard_map(shards, mesh=mesh, in_specs=in_specs, out_specs=out_specs, check_vma=False)
```
